512 devices in a mesh: dp: 32 (over z, x_lo), ctx: 16 (over y, x_hi, core).
Axes of the slice: x: 4 (x_hi: 2, x_lo: 2; x = x_hi * 2 + x_lo), y: 4, z: 16, core: 2. Of those that a mesh axis runs over, the one named last changes fastest.
Arguments:
- primal: bfloat16 [32, 2048, 2048], P('dp', 'ctx'), may hold values from -6 to 6
- tangent: bfloat16 [32, 2048, 2048], P('dp', 'ctx'), may hold values from -6 to 6
- cotangent: bfloat16 [32, 2048, 2048], P('dp', 'ctx'), may hold values from -6 to 6
- impulse: float32 [2048, 2048], P(None, 'ctx'), may hold values from -2 to 2
Outputs:
- out_primal: bfloat16 [32, 2048, 2048], P('dp', 'ctx')
- out_tangent: bfloat16 [32, 2048, 2048], P('dp', 'ctx')
- input_cotangent: bfloat16 [32, 2048, 2048], P('dp', 'ctx')
- impulse_grad: float32 [2048, 2048], P(None, 'ctx')
The draws below stay inside these ranges and needn't reach their ends.
All inputs are finite; a program needn't handle non-finite values.
Results may differ from the reference program's by a relative error of at most 0.001.
Values may be sent and summed in bfloat16 or wider, within the bound.
A program may use at most 128 MiB of HBM per device.

```python
import jax
import jax.numpy as jnp
from jax import lax

C = 2048
SEQ_LEN = 2048
SEQUENCES = 32


def draw_impulse(key, part):
    key = jax.random.fold_in(key, 7)
    rate_key, noise_key = jax.random.split(key)
    lowest = jnp.log(jnp.float32(30.0))
    highest = jnp.log(jnp.float32(4.0 * SEQ_LEN))
    spans = jnp.exp(jax.random.uniform(rate_key, (C,), jnp.float32, lowest, highest))
    places = jnp.arange(SEQ_LEN, dtype=jnp.float32)[:, None]
    noise = jnp.clip(jax.random.normal(noise_key, (SEQ_LEN, C), jnp.float32), -6.0, 6.0)
    return noise * jnp.sqrt(2.0 / spans)[None, :] * jnp.exp(-places / spans[None, :])


def shard_levels(stream_key, shape, cuts, least, high):
    def one(position, parts):
        heights = jax.random.uniform(jax.random.fold_in(jax.random.fold_in(stream_key, 6), position), (parts,), jnp.float32, least / len(cuts), high / len(cuts))
        return jnp.repeat(jnp.exp(heights), shape[position] // parts).reshape((-1,) + (1,) * (len(shape) - position - 1))

    gain = one(*cuts[0])
    for cut in cuts[1:]:
        gain = gain * one(*cut)
    return gain


def centred(rng, extent, scale, limit, cuts=(), kind=jnp.bfloat16):
    drawn = scale * jax.random.normal(rng, extent, jnp.float32)
    if cuts:
        drawn = drawn * shard_levels(rng, extent, cuts, -0.22, 0.18)
    return jnp.clip(drawn, -limit, limit).astype(kind)


def setup_inputs(seed: int = 0) -> dict:
    key_list = jax.random.split(jax.random.key(seed), 5)
    primal = centred(key_list[0], (SEQUENCES, SEQ_LEN, C), 1.0, 6.0, ((0, 32), (1, 16)))
    tangent = centred(key_list[1], (SEQUENCES, SEQ_LEN, C), 1.0, 6.0, ((0, 32), (1, 16)))
    cotangent = centred(key_list[2], (SEQUENCES, SEQ_LEN, C), 1.0, 6.0, ((0, 32), (1, 16)))
    impulse = draw_impulse(jax.random.fold_in(key_list[4], 71), 0)
    return {"primal": primal, "tangent": tangent, "cotangent": cotangent, "impulse": impulse}


def reference(primal, tangent, cotangent, impulse):
    total = 2 * SEQ_LEN
    filter_spec = jnp.fft.rfft(impulse, n=total, axis=0)

    def one_sequence(carry, pieces):
        seq_u, seq_du, seq_g = pieces
        spec_u = jnp.fft.rfft(seq_u.astype(jnp.float32), n=total, axis=0)
        spec_du = jnp.fft.rfft(seq_du.astype(jnp.float32), n=total, axis=0)
        spec_g = jnp.fft.rfft(seq_g.astype(jnp.float32), n=total, axis=0)
        result_u = jnp.fft.irfft(filter_spec * spec_u, n=total, axis=0)[:SEQ_LEN]
        result_du = jnp.fft.irfft(filter_spec * spec_du, n=total, axis=0)[:SEQ_LEN]
        result_g = jnp.fft.irfft(jnp.conj(filter_spec) * spec_g, n=total, axis=0)[:SEQ_LEN]
        partial_grad = jnp.fft.irfft(jnp.conj(spec_u) * spec_g, n=total, axis=0)[:SEQ_LEN]
        outs = (result_u.astype(jnp.bfloat16), result_du.astype(jnp.bfloat16), result_g.astype(jnp.bfloat16))
        return (carry + partial_grad, outs)
    start = jnp.zeros((SEQ_LEN, C), jnp.float32)
    summed, outs = lax.scan(one_sequence, start, (primal, tangent, cotangent))
    scale = 1.0 / jnp.sqrt(jnp.float32(SEQUENCES * SEQ_LEN))
    return (outs[0], outs[1], outs[2], summed * scale)
```

```python
import functools
import math

import jax
import jax.numpy as jnp
import ml_dtypes
import numpy as np
from jax import lax
from jax.experimental import pallas as pl
from jax.experimental.pallas import tpu as pltpu
from jax.sharding import PartitionSpec as P

MESH = pl.DeviceIdType.MESH
LANES = 128
SPLIT = 16
MIB = 1024 * 1024


def two_pieces(table):
    high = table.astype(ml_dtypes.bfloat16)
    low = (table - high.astype(np.float64)).astype(ml_dtypes.bfloat16)
    return high, low


def build_tables(length):
    total = 2 * length
    rows = length // SPLIT
    time = np.arange(rows)[None, :] * SPLIT + np.arange(SPLIT)[:, None]
    angle = 2.0 * np.pi * (time[:, None, :] * np.arange(rows)[None, :, None] % total) / total
    real, imag = np.cos(angle), -np.sin(angle)
    real[:, 0, :] = 1.0
    imag[:, 0, :] = 1.0 - 2.0 * (np.arange(rows) % 2)
    high, low = two_pieces(np.concatenate([real, imag], 1))
    analysis = np.concatenate([high, low], 2)
    real, imag = np.cos(angle) * (2.0 / total), -np.sin(angle) * (2.0 / total)
    real[:, 0, :] = (np.arange(rows) % 2 == 0)[None, :]
    imag[:, 0, :] = (np.arange(rows) % 2 == 1)[None, :]
    high, low = two_pieces(np.concatenate([real, imag], 1).transpose(0, 2, 1))
    synthesis = np.concatenate([high, low], 1)
    edge = np.zeros((2 * SPLIT, 2 * SPLIT))
    back = np.zeros((2 * SPLIT, 2 * SPLIT))
    point = np.arange(SPLIT)
    folded = np.arange(2 * SPLIT)
    for m in range(SPLIT):
        turn = 2.0 * np.pi * m * point / (2 * SPLIT)
        start = SPLIT * (m % 2)
        edge[m, start : start + SPLIT] = np.cos(turn)
        full = 2.0 * np.pi * m * folded / (2 * SPLIT)
        if m:
            edge[SPLIT + m, start : start + SPLIT] = -np.sin(turn)
            back[:, m] = 2.0 * np.cos(full) / total
            back[:, SPLIT + m] = -2.0 * np.sin(full) / total
    edge[SPLIT, :SPLIT] = np.cos(np.pi * point)
    back[:, 0] = 1.0 / total
    back[:, SPLIT] = np.cos(np.pi * folded) / total
    return analysis, synthesis, edge.astype(np.float32), back.astype(np.float32)


def times(value, power, sign):
    re, im = value
    power = (power * sign) % 16
    if power == 0:
        return (re, im)
    if power == 4:
        return (-im, re)
    if power == 8:
        return (-re, -im)
    if power == 12:
        return (im, -re)
    c, s = math.cos(math.pi * power / 8), math.sin(math.pi * power / 8)
    if power % 4 == 2:
        size = math.sqrt(0.5)
        if power == 2:
            return ((re - im) * size, (re + im) * size)
        if power == 6:
            return ((re + im) * -size, (re - im) * size)
        if power == 10:
            return ((im - re) * size, (re + im) * -size)
        return ((re + im) * size, (im - re) * size)
    return (re * c - im * s, re * s + im * c)


def four(a, b, c, d, sign):
    sr, si = a[0] + c[0], a[1] + c[1]
    dr, di = a[0] - c[0], a[1] - c[1]
    tr, ti = b[0] + d[0], b[1] + d[1]
    er, ei = b[0] - d[0], b[1] - d[1]
    plus = (dr - ei, di + er)
    minus = (dr + ei, di - er)
    if sign < 0:
        plus, minus = minus, plus
    return ((sr + tr, si + ti), plus, (sr - tr, si - ti), minus)


def sixteen(points, sign):
    inner = [four(points[b], points[4 + b], points[8 + b], points[12 + b], sign) for b in range(4)]
    result = [None] * 16
    for c in range(4):
        column = [times(inner[b][c], b * c, sign) for b in range(4)]
        outer = four(*column, sign)
        for d in range(4):
            result[c + 4 * d] = outer[d]
    return result


def product(a, b, conjugate):
    if conjugate:
        return (a[0] * b[0] + a[1] * b[1], a[0] * b[1] - a[1] * b[0])
    return (a[0] * b[0] - a[1] * b[1], a[0] * b[1] + a[1] * b[0])


U, DU, G, H = range(4)
PAIRS = ((H, U, False), (H, DU, False), (H, G, True), (U, G, True))


def lanes(index):
    return slice(index * LANES, (index + 1) * LANES)


def transform_kernel(
    u_ref, du_ref, g_ref, h_ref, analysis, synthesis, edge, back,
    ou_ref, odu_ref, og_ref, grad_ref,
    signal, spec, prod, rim, rim_out,
):
    length = h_ref.shape[0]
    rows = length // SPLIT
    signal[U] = u_ref[...].astype(jnp.float32)
    signal[DU] = du_ref[...].astype(jnp.float32)
    signal[G] = g_ref[...].astype(jnp.float32)
    high = h_ref[...].astype(jnp.bfloat16).astype(jnp.float32)
    signal[H] = high
    signal[H + 1] = h_ref[...] - high

    for q in range(SPLIT):
        pieces = [signal[s, pl.ds(q, rows, stride=SPLIT), :].astype(jnp.bfloat16) for s in range(5)]
        block = jnp.concatenate(pieces, 1)
        block = jnp.concatenate([block, block], 0)
        out = jnp.dot(analysis[q], block, preferred_element_type=jnp.float32)
        parts = [out[:, lanes(s)] for s in range(3)] + [out[:, lanes(3)] + out[:, lanes(4)]]
        for s in range(4):
            spec[s, q] = parts[s]
            rim[q : q + 1, lanes(s)] = parts[s][0:1]
            rim[SPLIT + q : SPLIT + q + 1, lanes(s)] = parts[s][rows : rows + 1]

    rims = jnp.dot(
        edge[...], rim[...], precision=lax.Precision.HIGHEST, preferred_element_type=jnp.float32
    )
    first = lax.broadcasted_iota(jnp.int32, (SPLIT, LANES), 0) == 0
    for o, (a, b, conjugate) in enumerate(PAIRS):
        left = (rims[:SPLIT, lanes(a)], rims[SPLIT:, lanes(a)])
        right = (rims[:SPLIT, lanes(b)], rims[SPLIT:, lanes(b)])
        re, im = product(left, right, conjugate)
        rim[:SPLIT, lanes(o)] = jnp.where(first, left[0] * right[0], re)
        rim[SPLIT:, lanes(o)] = jnp.where(first, left[1] * right[1], im)
    rim_out[...] = jnp.dot(
        back[...], rim[...], precision=lax.Precision.HIGHEST, preferred_element_type=jnp.float32
    )

    @pl.loop(0, rows // 8)
    def _(tile):
        upper = pl.ds(pl.multiple_of(tile * 8, 8), 8)
        lower = pl.ds(pl.multiple_of(rows + tile * 8, 8), 8)
        for s in range(4):
            found = sixteen([(spec[s, q, upper, :], spec[s, q, lower, :]) for q in range(SPLIT)], -1)
            for j in range(SPLIT):
                spec[s, j, upper, :] = found[j][0]
                spec[s, j, lower, :] = found[j][1]
        for o, (a, b, conjugate) in enumerate(PAIRS):
            mixed = [
                product(
                    (spec[a, j, upper, :], spec[a, j, lower, :]),
                    (spec[b, j, upper, :], spec[b, j, lower, :]),
                    conjugate,
                )
                for j in range(SPLIT)
            ]
            found = sixteen(mixed, 1)
            for q in range(SPLIT):
                prod[o, q, upper, :] = found[q][0]
                prod[o, q, lower, :] = found[q][1]

    for q in range(SPLIT):
        for o in range(4):
            prod[o, q, 0:1, :] = rim_out[q : q + 1, lanes(o)]
            prod[o, q, rows : rows + 1, :] = rim_out[SPLIT + q : SPLIT + q + 1, lanes(o)]

    for q in range(SPLIT):
        block = jnp.concatenate([prod[o, q] for o in range(4)], 1)
        top = block.astype(jnp.bfloat16)
        rest = (block - top.astype(jnp.float32)).astype(jnp.bfloat16)
        both = jnp.dot(synthesis[q], top, preferred_element_type=jnp.float32)
        more = jnp.dot(synthesis[q, :rows], rest, preferred_element_type=jnp.float32)
        out = both[:rows] + (both[rows:] + more)
        for o in range(4):
            signal[o, pl.ds(q, rows, stride=SPLIT), :] = out[:, lanes(o)]

    ou_ref[...] = signal[U].astype(jnp.bfloat16)
    odu_ref[...] = signal[DU].astype(jnp.bfloat16)
    og_ref[...] = signal[G].astype(jnp.bfloat16)
    grad_ref[...] = signal[3]


def transform(u, du, g, h, tables):
    length, width = h.shape
    rows = length // SPLIT
    whole = pl.BlockSpec(memory_space=pltpu.VMEM)
    half = jax.ShapeDtypeStruct((length, width), jnp.bfloat16)
    return pl.pallas_call(
        transform_kernel,
        out_shape=(half, half, half, jax.ShapeDtypeStruct((length, width), jnp.float32)),
        in_specs=[whole] * 8,
        out_specs=(whole,) * 4,
        scratch_shapes=[
            pltpu.VMEM((5, length, width), jnp.float32),
            pltpu.VMEM((4, SPLIT, 2 * rows, width), jnp.float32),
            pltpu.VMEM((4, SPLIT, 2 * rows, width), jnp.float32),
            pltpu.VMEM((2 * SPLIT, 4 * width), jnp.float32),
            pltpu.VMEM((2 * SPLIT, 4 * width), jnp.float32),
        ],
        compiler_params=pltpu.CompilerParams(vmem_limit_bytes=48 * MIB),
        name="transform",
    )(u, du, g, h, *tables)


def gather_kernel(n, a_ref, b_ref, c_ref, oa_ref, ob_ref, oc_ref, local_sem, send_sem, recv_sem):
    me = lax.axis_index("ctx")
    barrier = pltpu.get_barrier_semaphore()
    for step in range(1, n):
        pl.semaphore_signal(
            barrier, inc=1, device_id={"ctx": lax.rem(me + step, n)}, device_id_type=MESH
        )
    pl.semaphore_wait(barrier, n - 1)
    tokens = a_ref.shape[1]
    mine = pl.ds(pl.multiple_of(me * tokens, tokens), tokens)
    own = pl.ds(pl.multiple_of(me * LANES, LANES), LANES)
    copies = []
    for i, (src, dst) in enumerate(((a_ref, oa_ref), (b_ref, ob_ref), (c_ref, oc_ref))):
        for step in range(1, n):
            other = lax.rem(me + step, n)
            copy = pltpu.make_async_remote_copy(
                src_ref=src.at[0, :, pl.ds(pl.multiple_of(other * LANES, LANES), LANES)],
                dst_ref=dst.at[mine, :],
                send_sem=send_sem.at[i, step],
                recv_sem=recv_sem.at[i, step],
                device_id={"ctx": other},
                device_id_type=MESH,
            )
            copy.start()
            copies.append(copy)
        copy = pltpu.make_async_copy(src.at[0, :, own], dst.at[mine, :], local_sem.at[i])
        copy.start()
        copies.append(copy)
    for copy in copies:
        copy.wait()


def gather_tokens(a, b, c):
    n = lax.axis_size("ctx")
    length = n * a.shape[1]
    anywhere = pl.BlockSpec(memory_space=pl.ANY)
    shape = jax.ShapeDtypeStruct((length, LANES), jnp.bfloat16)
    return pl.pallas_call(
        functools.partial(gather_kernel, n),
        out_shape=(shape,) * 3,
        in_specs=[anywhere] * 3,
        out_specs=(anywhere,) * 3,
        scratch_shapes=[
            pltpu.SemaphoreType.DMA((3,)),
            pltpu.SemaphoreType.DMA((3, n)),
            pltpu.SemaphoreType.DMA((3, n)),
        ],
        compiler_params=pltpu.CompilerParams(collective_id=0, has_side_effects=True),
        name="gather_tokens",
    )(a, b, c)


def scatter_kernel(
    n, rings, a_ref, b_ref, c_ref, part_ref, oa_ref, ob_ref, oc_ref, grad_ref,
    right_box, left_box, pair_out, pair_in,
    local_sem, send_sem, recv_sem, right_send, right_recv, left_send, left_recv, pair_sem,
    right_send2, right_recv2, left_send2, left_recv2,
):
    me = lax.axis_index("ctx")
    dp = lax.axis_index("dp")
    z, x = lax.div(dp, 2), lax.rem(dp, 2)
    up = {"dp": lax.rem(z + 1, rings) * 2 + x}
    down = {"dp": lax.rem(z + rings - 1, rings) * 2 + x}
    twin = {"dp": z * 2 + 1 - x}
    barrier = pltpu.get_barrier_semaphore()
    for step in range(1, n):
        pl.semaphore_signal(
            barrier, inc=1, device_id={"ctx": lax.rem(me + step, n)}, device_id_type=MESH
        )
    for device in (up, down, twin):
        pl.semaphore_signal(barrier, inc=1, device_id=device, device_id_type=MESH)
    pl.semaphore_wait(barrier, n + 2)

    tokens = oa_ref.shape[1]
    rows = part_ref.shape[0] // rings
    far, near = rings // 2, rings // 2 - 1

    def chunk(index):
        place = lax.rem(index + 2 * rings, rings)
        return pl.ds(pl.multiple_of(place * rows, rows), rows)

    def send(src, dst, sends, recvs, step, device):
        copy = pltpu.make_async_remote_copy(
            src_ref=src, dst_ref=dst, send_sem=sends.at[step], recv_sem=recvs.at[step],
            device_id=device, device_id_type=MESH,
        )
        copy.start()
        return copy

    started = []
    right = send(part_ref.at[chunk(z + far), :], right_box.at[0], right_send, right_recv, 0, up)
    left = send(part_ref.at[chunk(z - near), :], left_box.at[0], left_send, left_recv, 0, down)
    started += [right, left]

    own = pl.ds(pl.multiple_of(me * LANES, LANES), LANES)
    mine = pl.ds(pl.multiple_of(me * tokens, tokens), tokens)
    copies = []
    for i, (src, dst) in enumerate(((a_ref, oa_ref), (b_ref, ob_ref), (c_ref, oc_ref))):
        for step in range(1, n):
            other = lax.rem(me + step, n)
            copy = pltpu.make_async_remote_copy(
                src_ref=src.at[pl.ds(pl.multiple_of(other * tokens, tokens), tokens), :],
                dst_ref=dst.at[0, :, own],
                send_sem=send_sem.at[i, step],
                recv_sem=recv_sem.at[i, step],
                device_id={"ctx": other},
                device_id_type=MESH,
            )
            copy.start()
            copies.append(copy)
        copy = pltpu.make_async_copy(src.at[mine, :], dst.at[0, :, own], local_sem.at[i])
        copy.start()
        copies.append(copy)

    for step in range(1, far):
        right.wait_recv()
        right_box[step - 1] += part_ref[chunk(z + far - step), :]
        right = send(right_box.at[step - 1], right_box.at[step], right_send, right_recv, step, up)
        started.append(right)
        if step < near:
            left.wait_recv()
            left_box[step - 1] += part_ref[chunk(z - near + step), :]
            left = send(left_box.at[step - 1], left_box.at[step], left_send, left_recv, step, down)
            started.append(left)
    left.wait_recv()
    right.wait_recv()
    pair_out[...] = part_ref[chunk(z), :] + (right_box[far - 1] + left_box[near - 1])
    pair = pltpu.make_async_remote_copy(
        src_ref=pair_out, dst_ref=pair_in, send_sem=pair_sem.at[0], recv_sem=pair_sem.at[1],
        device_id=twin, device_id_type=MESH,
    )
    pair.start()
    pair.wait_recv()
    grad_ref[chunk(z), :] = pair_out[...] + pair_in[...]
    for step in range(far):
        if step:
            right.wait_recv()
        place = chunk(z - step)
        right = send(grad_ref.at[place, :], grad_ref.at[place, :], right_send2, right_recv2, step, up)
        started.append(right)
        if step < near:
            if step:
                left.wait_recv()
            place = chunk(z + step)
            left = send(grad_ref.at[place, :], grad_ref.at[place, :], left_send2, left_recv2, step, down)
            started.append(left)
    right.wait_recv()
    left.wait_recv()
    pair.wait_send()
    for copy in started:
        copy.wait_send()
    for copy in copies:
        copy.wait()


def scatter_tokens(a, b, c, part):
    n = lax.axis_size("ctx")
    rings = lax.axis_size("dp") // 2
    length, width = part.shape
    far, near = rings // 2, rings // 2 - 1
    anywhere = pl.BlockSpec(memory_space=pl.ANY)
    whole = pl.BlockSpec(memory_space=pltpu.VMEM)
    shape = jax.ShapeDtypeStruct((1, length // n, n * width), jnp.bfloat16)
    box = (length // rings, width)
    sem = pltpu.SemaphoreType.DMA
    return pl.pallas_call(
        functools.partial(scatter_kernel, n, rings),
        out_shape=(shape,) * 3 + (jax.ShapeDtypeStruct((length, width), jnp.float32),),
        in_specs=[anywhere] * 3 + [whole],
        out_specs=(anywhere,) * 3 + (whole,),
        scratch_shapes=[
            pltpu.VMEM((far,) + box, jnp.float32),
            pltpu.VMEM((near,) + box, jnp.float32),
            pltpu.VMEM(box, jnp.float32),
            pltpu.VMEM(box, jnp.float32),
            sem((3,)), sem((3, n)), sem((3, n)),
            sem((far,)), sem((far,)), sem((near,)), sem((near,)), sem((2,)),
            sem((far,)), sem((far,)), sem((near,)), sem((near,)),
        ],
        compiler_params=pltpu.CompilerParams(
            collective_id=1, has_side_effects=True, vmem_limit_bytes=32 * MIB
        ),
        name="scatter_tokens",
    )(a, b, c, part)


def local(primal, tangent, cotangent, impulse):
    length = impulse.shape[0]
    tables = [jnp.asarray(t) for t in build_tables(length)]
    u, g, du = gather_tokens(primal, cotangent, tangent)
    out_u, out_du, out_g, part = transform(u, du, g, impulse, tables)
    back_u, back_du, back_g, summed = scatter_tokens(out_u, out_du, out_g, part)
    scale = 1.0 / math.sqrt(lax.axis_size("dp") * length)
    return (back_u, back_du, back_g, summed * scale)


def solution(mesh):
    placed = (P("dp", "ctx", None), P("dp", "ctx", None), P("dp", "ctx", None), P(None, "ctx"))
    return jax.shard_map(
        local,
        mesh=mesh,
        in_specs=placed,
        out_specs=(
            P("dp", "ctx", None),
            P("dp", "ctx", None),
            P("dp", "ctx", None),
            P(None, "ctx"),
        ),
        check_vma=False,
    )
```

```python
import functools
import math

import jax
import jax.numpy as jnp
import ml_dtypes
import numpy as np
from jax import lax
from jax.experimental import pallas as pl
from jax.experimental.pallas import tpu as pltpu
from jax.sharding import PartitionSpec as P

MESH = pl.DeviceIdType.MESH
LANES = 128
SPLIT = 16
MIB = 1024 * 1024
UNROLL = 4


def two_pieces(table):
    high = table.astype(ml_dtypes.bfloat16)
    low = (table - high.astype(np.float64)).astype(ml_dtypes.bfloat16)
    return high, low


def build_tables(length):
    total = 2 * length
    rows = length // SPLIT
    time = np.arange(rows)[None, :] * SPLIT + np.arange(SPLIT)[:, None]
    angle = 2.0 * np.pi * (time[:, None, :] * np.arange(rows)[None, :, None] % total) / total
    real, imag = np.cos(angle), -np.sin(angle)
    real[:, 0, :] = 1.0
    imag[:, 0, :] = 1.0 - 2.0 * (np.arange(rows) % 2)
    high, low = two_pieces(np.concatenate([real, imag], 1))
    analysis = np.concatenate([high, low], 2)
    real, imag = np.cos(angle) * (2.0 / total), -np.sin(angle) * (2.0 / total)
    real[:, 0, :] = (np.arange(rows) % 2 == 0)[None, :]
    imag[:, 0, :] = (np.arange(rows) % 2 == 1)[None, :]
    high, low = two_pieces(np.concatenate([real, imag], 1).transpose(0, 2, 1))
    synthesis = np.concatenate([high, low], 1)
    edge = np.zeros((2 * SPLIT, 2 * SPLIT))
    back = np.zeros((2 * SPLIT, 2 * SPLIT))
    point = np.arange(SPLIT)
    folded = np.arange(2 * SPLIT)
    for m in range(SPLIT):
        turn = 2.0 * np.pi * m * point / (2 * SPLIT)
        start = SPLIT * (m % 2)
        edge[m, start : start + SPLIT] = np.cos(turn)
        full = 2.0 * np.pi * m * folded / (2 * SPLIT)
        if m:
            edge[SPLIT + m, start : start + SPLIT] = -np.sin(turn)
            back[:, m] = 2.0 * np.cos(full) / total
            back[:, SPLIT + m] = -2.0 * np.sin(full) / total
    edge[SPLIT, :SPLIT] = np.cos(np.pi * point)
    back[:, 0] = 1.0 / total
    back[:, SPLIT] = np.cos(np.pi * folded) / total
    return analysis, synthesis, edge.astype(np.float32), back.astype(np.float32)


def times(value, power, sign):
    re, im = value
    power = (power * sign) % 16
    if power == 0:
        return (re, im)
    if power == 4:
        return (-im, re)
    if power == 8:
        return (-re, -im)
    if power == 12:
        return (im, -re)
    c, s = math.cos(math.pi * power / 8), math.sin(math.pi * power / 8)
    if power % 4 == 2:
        size = math.sqrt(0.5)
        if power == 2:
            return ((re - im) * size, (re + im) * size)
        if power == 6:
            return ((re + im) * -size, (re - im) * size)
        if power == 10:
            return ((im - re) * size, (re + im) * -size)
        return ((re + im) * size, (im - re) * size)
    return (re * c - im * s, re * s + im * c)


def four(a, b, c, d, sign):
    sr, si = a[0] + c[0], a[1] + c[1]
    dr, di = a[0] - c[0], a[1] - c[1]
    tr, ti = b[0] + d[0], b[1] + d[1]
    er, ei = b[0] - d[0], b[1] - d[1]
    plus = (dr - ei, di + er)
    minus = (dr + ei, di - er)
    if sign < 0:
        plus, minus = minus, plus
    return ((sr + tr, si + ti), plus, (sr - tr, si - ti), minus)


def sixteen(points, sign):
    inner = [four(points[b], points[4 + b], points[8 + b], points[12 + b], sign) for b in range(4)]
    result = [None] * 16
    for c in range(4):
        column = [times(inner[b][c], b * c, sign) for b in range(4)]
        outer = four(*column, sign)
        for d in range(4):
            result[c + 4 * d] = outer[d]
    return result


def product(a, b, conjugate):
    if conjugate:
        return (a[0] * b[0] + a[1] * b[1], a[0] * b[1] - a[1] * b[0])
    return (a[0] * b[0] - a[1] * b[1], a[0] * b[1] + a[1] * b[0])


U, G, DU, H = range(4)
GRAD = 3
SUBS = 2


def fused_kernel(
    n, rings,
    u_ref, g_ref, du_ref, h_ref, analysis_ref, synthesis_ref, edge, back,
    ou_ref, og_ref, odu_ref, grad_ref,
    arrive, leave, impulse, analysis, synthesis, signal, spec, prod, rim, rim_spec, rim_mix, rim_out,
    part, right_box, left_box, pair_out, pair_in, total,
    table_sem, local_sem, in_send, in_recv, out_send, out_recv, sum_send, sum_recv, pair_sem, all_send, all_recv,
):
    me, dp = lax.axis_index("ctx"), lax.axis_index("dp")
    z, x = lax.div(dp, 2), lax.rem(dp, 2)
    up = {"dp": lax.rem(z + 1, rings) * 2 + x}
    down = {"dp": lax.rem(z + rings - 1, rings) * 2 + x}
    twin = {"dp": z * 2 + 1 - x}
    length = impulse.shape[0]
    rows = length // SPLIT
    tokens = length // n
    far, near = rings // 2, rings // 2 - 1
    sub = rows // SUBS
    mine = pl.ds(pl.multiple_of(me * tokens, tokens), tokens)
    own = pl.ds(pl.multiple_of(me * LANES, LANES), LANES)

    tables = [
        pltpu.make_async_copy(src, dst, table_sem.at[i])
        for i, (src, dst) in enumerate(((h_ref, impulse), (analysis_ref, analysis), (synthesis_ref, synthesis)))
    ]
    for copy in tables:
        copy.start()
    barrier = pltpu.get_barrier_semaphore()
    for step in range(1, n):
        pl.semaphore_signal(
            barrier, inc=1, device_id={"ctx": lax.rem(me + step, n)}, device_id_type=MESH
        )
    for device in (up, down, twin):
        pl.semaphore_signal(barrier, inc=1, device_id=device, device_id_type=MESH)
    pl.semaphore_wait(barrier, n + 2)

    remote, sent, locals_ = {}, [], {}

    def send_in(s):
        src = (u_ref, g_ref, du_ref)[s]
        remote[s] = []
        for step in range(1, n):
            other = lax.rem(me + step, n)
            copy = pltpu.make_async_remote_copy(
                src_ref=src.at[0, :, pl.ds(pl.multiple_of(other * LANES, LANES), LANES)],
                dst_ref=arrive.at[s, mine, :],
                send_sem=in_send.at[s, step], recv_sem=in_recv.at[s, step],
                device_id={"ctx": other}, device_id_type=MESH,
            )
            copy.start()
            remote[s].append(copy)
        locals_[s] = pltpu.make_async_copy(src.at[0, :, own], arrive.at[s, mine, :], local_sem.at[s])
        locals_[s].start()

    def receive(s):
        for copy in remote[s]:
            copy.wait_recv()
        locals_[s].wait()
        sent.extend(remote[s])

    finished = []

    def send_out(o):
        dst = (ou_ref, og_ref, odu_ref)[o]
        for step in range(1, n):
            other = lax.rem(me + step, n)
            copy = pltpu.make_async_remote_copy(
                src_ref=leave.at[o, pl.ds(pl.multiple_of(other * tokens, tokens), tokens), :],
                dst_ref=dst.at[0, :, own],
                send_sem=out_send.at[o, step], recv_sem=out_recv.at[o, step],
                device_id={"ctx": other}, device_id_type=MESH,
            )
            copy.start()
            finished.append(copy)
        copy = pltpu.make_async_copy(leave.at[o, mine, :], dst.at[0, :, own], local_sem.at[3 + o])
        copy.start()
        finished.append(copy)

    def analyse(s, slots):
        def body(q, carry):
            pieces = [signal[i, pl.ds(q, rows, stride=SPLIT), :].astype(jnp.bfloat16) for i in slots]
            block = jnp.concatenate(pieces, 1) if len(slots) > 1 else pieces[0]
            block = jnp.concatenate([block, block], 0)
            out = jnp.dot(analysis[q], block, preferred_element_type=jnp.float32)
            if len(slots) > 1:
                out = out[:, :LANES] + out[:, LANES:]
            spec[s, q] = out
            rim[pl.ds(q, 1), :] = out[0:1]
            rim[pl.ds(SPLIT + q, 1), :] = out[rows : rows + 1]
            return carry

        lax.fori_loop(0, SPLIT, body, 0, unroll=UNROLL)
        rim_spec[s] = jnp.dot(
            edge[...], rim[...], precision=lax.Precision.HIGHEST, preferred_element_type=jnp.float32
        )

    def mix(o, a, b, conjugate, turned, kept):
        left, right = (rim_spec[a, :SPLIT], rim_spec[a, SPLIT:]), (rim_spec[b, :SPLIT], rim_spec[b, SPLIT:])
        re, im = product(left, right, conjugate)
        first = lax.broadcasted_iota(jnp.int32, (SPLIT, LANES), 0) == 0
        rim_mix[:SPLIT] = jnp.where(first, left[0] * right[0], re)
        rim_mix[SPLIT:] = jnp.where(first, left[1] * right[1], im)
        rim_out[o] = jnp.dot(
            back[...], rim_mix[...], precision=lax.Precision.HIGHEST, preferred_element_type=jnp.float32
        )

        def body(tile, carry):
            upper = pl.ds(pl.multiple_of(tile * 8, 8), 8)
            lower = pl.ds(pl.multiple_of(rows + tile * 8, 8), 8)
            points = [(spec[b, j, upper, :], spec[b, j, lower, :]) for j in range(SPLIT)]
            if not turned:
                points = sixteen(points, -1)
                if kept:
                    for j in range(SPLIT):
                        spec[b, j, upper, :] = points[j][0]
                        spec[b, j, lower, :] = points[j][1]
            points = [
                product((spec[a, j, upper, :], spec[a, j, lower, :]), points[j], conjugate)
                for j in range(SPLIT)
            ]
            points = sixteen(points, 1)
            for q in range(SPLIT):
                prod[o, q, upper, :] = points[q][0]
                prod[o, q, lower, :] = points[q][1]
            return carry

        lax.fori_loop(0, rows // 8, body, 0)

    def turn(s):
        def body(tile, carry):
            upper = pl.ds(pl.multiple_of(tile * 8, 8), 8)
            lower = pl.ds(pl.multiple_of(rows + tile * 8, 8), 8)
            points = sixteen([(spec[s, q, upper, :], spec[s, q, lower, :]) for q in range(SPLIT)], -1)
            for j in range(SPLIT):
                spec[s, j, upper, :] = points[j][0]
                spec[s, j, lower, :] = points[j][1]
            return carry

        lax.fori_loop(0, rows // 8, body, 0)

    def residue(o, q):
        prod[o, q, 0:1, :] = rim_out[o, pl.ds(q, 1), :]
        prod[o, q, rows : rows + 1, :] = rim_out[o, pl.ds(SPLIT + q, 1), :]
        block = prod[o, q]
        top = block.astype(jnp.bfloat16)
        rest = (block - top.astype(jnp.float32)).astype(jnp.bfloat16)
        both = jnp.dot(synthesis[q], top, preferred_element_type=jnp.float32)
        more = jnp.dot(synthesis[q, :rows], rest, preferred_element_type=jnp.float32)
        return both[:rows] + (both[rows:] + more)

    def finish(o):
        def body(q, carry):
            signal[o, pl.ds(q, rows, stride=SPLIT), :] = residue(o, q)
            return carry

        lax.fori_loop(0, SPLIT, body, 0, unroll=UNROLL)
        leave[o] = signal[o].astype(jnp.bfloat16)

    def load(s):
        signal[s] = arrive[s].astype(jnp.float32)

    def place(index):
        return lax.rem(index + 2 * rings, rings)

    started = []

    def hop(src, dst, sends, recvs, device):
        copy = pltpu.make_async_remote_copy(
            src_ref=src, dst_ref=dst, send_sem=sends, recv_sem=recvs, device_id=device, device_id_type=MESH
        )
        copy.start()
        started.append(copy)
        return copy

    cuts = [pl.ds(c * sub, sub) for c in range(SUBS)]

    send_in(U)
    send_in(G)
    tables[0].wait()
    high = impulse[...].astype(jnp.bfloat16).astype(jnp.float32)
    signal[0] = high
    signal[1] = impulse[...] - high
    tables[1].wait()
    analyse(H, (0, 1))
    turn(H)
    receive(U)
    load(U)
    analyse(U, (U,))
    mix(U, H, U, False, False, True)
    tables[2].wait()
    finish(U)
    receive(G)
    load(G)
    analyse(G, (G,))
    mix(GRAD, U, G, True, False, True)

    def chunk(q):
        part[q] = residue(GRAD, q)

    chunk(place(z + far))
    chunk(place(z - near))
    right = [
        hop(part.at[place(z + far), c], right_box.at[0, c], sum_send.at[0, 0, i], sum_recv.at[0, 0, i], up)
        for i, c in enumerate(cuts)
    ]
    left = [
        hop(part.at[place(z - near), c], left_box.at[0, c], sum_send.at[1, 0, i], sum_recv.at[1, 0, i], down)
        for i, c in enumerate(cuts)
    ]

    def others(step, carry):
        chunk(place(z - near + step))
        return carry

    lax.fori_loop(1, rings - 1, others, 0, unroll=2)
    send_out(U)
    send_in(DU)

    def last_product():
        receive(DU)
        load(DU)
        analyse(DU, (DU,))

    work = {
        1: lambda: mix(G, H, G, True, True, False),
        2: lambda: (finish(G), send_out(G)),
        4: last_product,
        5: lambda: mix(DU, H, DU, False, False, False),
        6: lambda: (finish(DU), send_out(DU)),
    }
    for step in range(1, far):
        for i, c in enumerate(cuts):
            right[i].wait_recv()
            right_box[step - 1, c] += part[place(z + far - step), c]
            right[i] = hop(
                right_box.at[step - 1, c], right_box.at[step, c],
                sum_send.at[0, step, i], sum_recv.at[0, step, i], up,
            )
            if step < near:
                left[i].wait_recv()
                left_box[step - 1, c] += part[place(z - near + step), c]
                left[i] = hop(
                    left_box.at[step - 1, c], left_box.at[step, c],
                    sum_send.at[1, step, i], sum_recv.at[1, step, i], down,
                )
        if step in work:
            work[step]()
    pair = []
    for i, c in enumerate(cuts):
        left[i].wait_recv()
        right[i].wait_recv()
        pair_out[c] = part[place(z), c] + (right_box[far - 1, c] + left_box[near - 1, c])
        pair.append(hop(pair_out.at[c], pair_in.at[c], pair_sem.at[0, i], pair_sem.at[1, i], twin))
    for step in range(far):
        for i, c in enumerate(cuts):
            if step:
                right[i].wait_recv()
            else:
                pair[i].wait_recv()
                total[z, c] = pair_out[c] + pair_in[c]
            here = total.at[place(z - step), c]
            right[i] = hop(here, here, all_send.at[0, step, i], all_recv.at[0, step, i], up)
            if step < near:
                if step:
                    left[i].wait_recv()
                here = total.at[place(z + step), c]
                left[i] = hop(here, here, all_send.at[1, step, i], all_recv.at[1, step, i], down)
    for i in range(SUBS):
        right[i].wait_recv()
        left[i].wait_recv()
    for q in range(SPLIT):
        grad_ref[pl.ds(q, rows, stride=SPLIT), :] = total[q]
    for copy in started + sent:
        copy.wait_send()
    for copy in finished:
        copy.wait()


def fused(u, g, du, h, tables):
    n = lax.axis_size("ctx")
    rings = lax.axis_size("dp") // 2
    length, width = h.shape
    rows = length // SPLIT
    far = rings // 2
    anywhere = pl.BlockSpec(memory_space=pl.ANY)
    whole = pl.BlockSpec(memory_space=pltpu.VMEM)
    shape = jax.ShapeDtypeStruct((1, length // n, n * width), jnp.bfloat16)
    sem = pltpu.SemaphoreType.DMA

    def space(*sizes, kind=jnp.float32):
        return pltpu.VMEM(sizes, kind)

    half = jnp.bfloat16
    return pl.pallas_call(
        functools.partial(fused_kernel, n, rings),
        out_shape=(shape,) * 3 + (jax.ShapeDtypeStruct((length, width), jnp.float32),),
        in_specs=[anywhere] * 6 + [whole] * 2,
        out_specs=(anywhere,) * 3 + (whole,),
        scratch_shapes=[
            space(3, length, width, kind=half),
            space(3, length, width, kind=half),
            space(length, width),
            space(*tables[0].shape, kind=half),
            space(*tables[1].shape, kind=half),
            space(3, length, width),
            space(4, SPLIT, 2 * rows, width),
            space(4, SPLIT, 2 * rows, width),
            space(2 * SPLIT, width),
            space(4, 2 * SPLIT, width),
            space(2 * SPLIT, width),
            space(4, 2 * SPLIT, width),
            space(rings, rows, width),
            space(far, rows, width),
            space(far, rows, width),
            space(rows, width),
            space(rows, width),
            space(rings, rows, width),
            sem((3,)), sem((6,)),
            sem((3, n)), sem((3, n)), sem((3, n)), sem((3, n)),
            sem((2, far, SUBS)), sem((2, far, SUBS)), sem((2, SUBS)),
            sem((2, far, SUBS)), sem((2, far, SUBS)),
        ],
        compiler_params=pltpu.CompilerParams(
            collective_id=0, has_side_effects=True, vmem_limit_bytes=48 * MIB
        ),
        name="hyena",
    )(u, g, du, h, *tables)


def local(primal, tangent, cotangent, impulse):
    length = impulse.shape[0]
    tables = [jnp.asarray(t) for t in build_tables(length)]
    back_u, back_g, back_du, summed = fused(primal, cotangent, tangent, impulse, tables)
    scale = 1.0 / math.sqrt(lax.axis_size("dp") * length)
    return (back_u, back_du, back_g, summed * scale)


def solution(mesh):
    placed = (P("dp", "ctx", None), P("dp", "ctx", None), P("dp", "ctx", None), P(None, "ctx"))
    return jax.shard_map(
        local,
        mesh=mesh,
        in_specs=placed,
        out_specs=(
            P("dp", "ctx", None),
            P("dp", "ctx", None),
            P("dp", "ctx", None),
            P(None, "ctx"),
        ),
        check_vma=False,
    )
```

```python
import functools
import math

import jax
import jax.numpy as jnp
import ml_dtypes
import numpy as np
from jax import lax
from jax.experimental import pallas as pl
from jax.experimental.pallas import tpu as pltpu
from jax.sharding import PartitionSpec as P

MESH = pl.DeviceIdType.MESH
LANES = 128
SPLIT = 16
MIB = 1024 * 1024
UNROLL = 16


def two_pieces(table):
    high = table.astype(ml_dtypes.bfloat16)
    low = (table - high.astype(np.float64)).astype(ml_dtypes.bfloat16)
    return high, low


def build_tables(length):
    total = 2 * length
    rows = length // SPLIT
    time = np.arange(rows)[None, :] * SPLIT + np.arange(SPLIT)[:, None]
    angle = 2.0 * np.pi * (time[:, None, :] * np.arange(rows)[None, :, None] % total) / total
    real, imag = np.cos(angle), -np.sin(angle)
    real[:, 0, :] = 1.0
    imag[:, 0, :] = 1.0 - 2.0 * (np.arange(rows) % 2)
    high, low = two_pieces(np.concatenate([real, imag], 1))
    analysis = np.concatenate([high, low], 2)
    real, imag = np.cos(angle) * (2.0 / total), -np.sin(angle) * (2.0 / total)
    real[:, 0, :] = (np.arange(rows) % 2 == 0)[None, :]
    imag[:, 0, :] = (np.arange(rows) % 2 == 1)[None, :]
    high, low = two_pieces(np.concatenate([real, imag], 1).transpose(0, 2, 1))
    synthesis = np.concatenate([high, low], 1)
    edge = np.zeros((2 * SPLIT, 2 * SPLIT))
    back = np.zeros((2 * SPLIT, 2 * SPLIT))
    point = np.arange(SPLIT)
    folded = np.arange(2 * SPLIT)
    for m in range(SPLIT):
        turn = 2.0 * np.pi * m * point / (2 * SPLIT)
        start = SPLIT * (m % 2)
        edge[m, start : start + SPLIT] = np.cos(turn)
        full = 2.0 * np.pi * m * folded / (2 * SPLIT)
        if m:
            edge[SPLIT + m, start : start + SPLIT] = -np.sin(turn)
            back[:, m] = 2.0 * np.cos(full) / total
            back[:, SPLIT + m] = -2.0 * np.sin(full) / total
    edge[SPLIT, :SPLIT] = np.cos(np.pi * point)
    back[:, 0] = 1.0 / total
    back[:, SPLIT] = np.cos(np.pi * folded) / total
    return analysis, synthesis, edge.astype(np.float32), back.astype(np.float32)


def times(value, power, sign):
    re, im = value
    power = (power * sign) % 16
    if power == 0:
        return (re, im)
    if power == 4:
        return (-im, re)
    if power == 8:
        return (-re, -im)
    if power == 12:
        return (im, -re)
    c, s = math.cos(math.pi * power / 8), math.sin(math.pi * power / 8)
    if power % 4 == 2:
        size = math.sqrt(0.5)
        if power == 2:
            return ((re - im) * size, (re + im) * size)
        if power == 6:
            return ((re + im) * -size, (re - im) * size)
        if power == 10:
            return ((im - re) * size, (re + im) * -size)
        return ((re + im) * size, (im - re) * size)
    return (re * c - im * s, re * s + im * c)


def four(a, b, c, d, sign):
    sr, si = a[0] + c[0], a[1] + c[1]
    dr, di = a[0] - c[0], a[1] - c[1]
    tr, ti = b[0] + d[0], b[1] + d[1]
    er, ei = b[0] - d[0], b[1] - d[1]
    plus = (dr - ei, di + er)
    minus = (dr + ei, di - er)
    if sign < 0:
        plus, minus = minus, plus
    return ((sr + tr, si + ti), plus, (sr - tr, si - ti), minus)


def sixteen(points, sign):
    inner = [four(points[b], points[4 + b], points[8 + b], points[12 + b], sign) for b in range(4)]
    result = [None] * 16
    for c in range(4):
        column = [times(inner[b][c], b * c, sign) for b in range(4)]
        outer = four(*column, sign)
        for d in range(4):
            result[c + 4 * d] = outer[d]
    return result


def product(a, b, conjugate):
    if conjugate:
        return (a[0] * b[0] + a[1] * b[1], a[0] * b[1] - a[1] * b[0])
    return (a[0] * b[0] - a[1] * b[1], a[0] * b[1] + a[1] * b[0])


U, G, DU, H = range(4)
GRAD = 3
SUBS = 2


def fused_kernel(
    n, rings, scale,
    u_ref, g_ref, du_ref, h_ref, analysis_ref, synthesis_ref, edge, back,
    ou_ref, og_ref, odu_ref, grad_ref,
    arrive, leave, impulse, analysis, synthesis, signal, spec, prod, rim, rim_spec, rim_mix, rim_out,
    part, right_box, left_box, right_leaf, left_leaf, landing, total,
    table_sem, local_sem, in_send, in_recv, out_send, out_recv, sum_send, sum_recv, leaf_send, leaf_recv, land_send, land_recv,
    all_send, all_recv, near_send, near_recv, twin_send, twin_recv,
):
    me, dp = lax.axis_index("ctx"), lax.axis_index("dp")
    z, x = lax.div(dp, 2), lax.rem(dp, 2)
    up, up_two, down, down_two = (
        {"dp": lax.rem(z + move, rings) * 2 + x} for move in (1, 2, rings - 1, rings - 2)
    )
    twin = {"dp": z * 2 + 1 - x}
    around = [
        {"dp": lax.rem(z + move, rings) * 2 + 1 - x} for move in (1, 2, rings - 1, rings - 2)
    ]
    length = impulse.shape[0]
    rows = length // SPLIT
    tokens = length // n
    steps = rings // 4
    sub = rows // SUBS
    mine = pl.ds(pl.multiple_of(me * tokens, tokens), tokens)
    own = pl.ds(pl.multiple_of(me * LANES, LANES), LANES)

    tables = [
        pltpu.make_async_copy(src, dst, table_sem.at[i])
        for i, (src, dst) in enumerate(((h_ref, impulse), (analysis_ref, analysis), (synthesis_ref, synthesis)))
    ]
    for copy in tables:
        copy.start()
    barrier = pltpu.get_barrier_semaphore()
    for step in range(1, n):
        pl.semaphore_signal(
            barrier, inc=1, device_id={"ctx": lax.rem(me + step, n)}, device_id_type=MESH
        )
    for device in (up, up_two, down, down_two, twin, *around):
        pl.semaphore_signal(barrier, inc=1, device_id=device, device_id_type=MESH)
    pl.semaphore_wait(barrier, n + 8)

    remote, sent, locals_ = {}, [], {}

    def send_in(s):
        src = (u_ref, g_ref, du_ref)[s]
        remote[s] = []
        for step in range(1, n):
            other = lax.rem(me + step, n)
            copy = pltpu.make_async_remote_copy(
                src_ref=src.at[0, :, pl.ds(pl.multiple_of(other * LANES, LANES), LANES)],
                dst_ref=arrive.at[s, mine, :],
                send_sem=in_send.at[s, step], recv_sem=in_recv.at[s, step],
                device_id={"ctx": other}, device_id_type=MESH,
            )
            copy.start()
            remote[s].append(copy)
        locals_[s] = pltpu.make_async_copy(src.at[0, :, own], arrive.at[s, mine, :], local_sem.at[s])
        locals_[s].start()

    def receive(s):
        for copy in remote[s]:
            copy.wait_recv()
        locals_[s].wait()
        sent.extend(remote[s])

    finished = []

    def send_out(o):
        dst = (ou_ref, og_ref, odu_ref)[o]
        for step in range(1, n):
            other = lax.rem(me + step, n)
            copy = pltpu.make_async_remote_copy(
                src_ref=leave.at[o, pl.ds(pl.multiple_of(other * tokens, tokens), tokens), :],
                dst_ref=dst.at[0, :, own],
                send_sem=out_send.at[o, step], recv_sem=out_recv.at[o, step],
                device_id={"ctx": other}, device_id_type=MESH,
            )
            copy.start()
            finished.append(copy)
        copy = pltpu.make_async_copy(leave.at[o, mine, :], dst.at[0, :, own], local_sem.at[3 + o])
        copy.start()
        finished.append(copy)

    def analyse(s, slots):
        def body(q, carry):
            pieces = [signal[i, pl.ds(q, rows, stride=SPLIT), :].astype(jnp.bfloat16) for i in slots]
            block = jnp.concatenate(pieces, 1) if len(slots) > 1 else pieces[0]
            block = jnp.concatenate([block, block], 0)
            out = jnp.dot(analysis[q], block, preferred_element_type=jnp.float32)
            if len(slots) > 1:
                out = out[:, :LANES] + out[:, LANES:]
            spec[s, q] = out
            rim[pl.ds(q, 1), :] = out[0:1]
            rim[pl.ds(SPLIT + q, 1), :] = out[rows : rows + 1]
            return carry

        lax.fori_loop(0, SPLIT, body, 0, unroll=UNROLL)
        rim_spec[s] = jnp.dot(
            edge[...], rim[...], precision=lax.Precision.HIGHEST, preferred_element_type=jnp.float32
        )

    def mix(o, a, b, conjugate, turned, kept):
        left, right = (rim_spec[a, :SPLIT], rim_spec[a, SPLIT:]), (rim_spec[b, :SPLIT], rim_spec[b, SPLIT:])
        re, im = product(left, right, conjugate)
        first = lax.broadcasted_iota(jnp.int32, (SPLIT, LANES), 0) == 0
        rim_mix[:SPLIT] = jnp.where(first, left[0] * right[0], re)
        rim_mix[SPLIT:] = jnp.where(first, left[1] * right[1], im)
        rim_out[o] = jnp.dot(
            back[...], rim_mix[...], precision=lax.Precision.HIGHEST, preferred_element_type=jnp.float32
        )

        def body(tile, carry):
            upper = pl.ds(pl.multiple_of(tile * 8, 8), 8)
            lower = pl.ds(pl.multiple_of(rows + tile * 8, 8), 8)
            points = [(spec[b, j, upper, :], spec[b, j, lower, :]) for j in range(SPLIT)]
            if not turned:
                points = sixteen(points, -1)
                if kept:
                    for j in range(SPLIT):
                        spec[b, j, upper, :] = points[j][0]
                        spec[b, j, lower, :] = points[j][1]
            points = [
                product((spec[a, j, upper, :], spec[a, j, lower, :]), points[j], conjugate)
                for j in range(SPLIT)
            ]
            points = sixteen(points, 1)
            for q in range(SPLIT):
                prod[o, q, upper, :] = points[q][0]
                prod[o, q, lower, :] = points[q][1]
            return carry

        lax.fori_loop(0, rows // 8, body, 0)

    def turn(s):
        def body(tile, carry):
            upper = pl.ds(pl.multiple_of(tile * 8, 8), 8)
            lower = pl.ds(pl.multiple_of(rows + tile * 8, 8), 8)
            points = sixteen([(spec[s, q, upper, :], spec[s, q, lower, :]) for q in range(SPLIT)], -1)
            for j in range(SPLIT):
                spec[s, j, upper, :] = points[j][0]
                spec[s, j, lower, :] = points[j][1]
            return carry

        lax.fori_loop(0, rows // 8, body, 0)

    def residue(o, q):
        prod[o, q, 0:1, :] = rim_out[o, pl.ds(q, 1), :]
        prod[o, q, rows : rows + 1, :] = rim_out[o, pl.ds(SPLIT + q, 1), :]
        block = prod[o, q]
        top = block.astype(jnp.bfloat16)
        rest = (block - top.astype(jnp.float32)).astype(jnp.bfloat16)
        both = jnp.dot(synthesis[q], top, preferred_element_type=jnp.float32)
        more = jnp.dot(synthesis[q, :rows], rest, preferred_element_type=jnp.float32)
        return both[:rows] + (both[rows:] + more)

    def finish(o):
        def body(q, carry):
            signal[o, pl.ds(q, rows, stride=SPLIT), :] = residue(o, q)
            return carry

        lax.fori_loop(0, SPLIT, body, 0, unroll=UNROLL)
        leave[o] = signal[o].astype(jnp.bfloat16)

    def load(s):
        signal[s] = arrive[s].astype(jnp.float32)

    def place(index):
        return lax.rem(index + 2 * rings, rings)

    started = []

    def hop(src, dst, sends, recvs, device):
        copy = pltpu.make_async_remote_copy(
            src_ref=src, dst_ref=dst, send_sem=sends, recv_sem=recvs, device_id=device, device_id_type=MESH
        )
        copy.start()
        started.append(copy)
        return copy

    cuts = [pl.ds(c * sub, sub) for c in range(SUBS)]

    send_in(U)
    send_in(G)
    tables[0].wait()
    high = impulse[...].astype(jnp.bfloat16).astype(jnp.float32)
    signal[0] = high
    signal[1] = impulse[...] - high
    tables[1].wait()
    analyse(H, (0, 1))
    turn(H)
    receive(U)
    load(U)
    analyse(U, (U,))
    turn(U)
    receive(G)
    load(G)
    analyse(G, (G,))
    mix(GRAD, U, G, True, False, True)
    tables[2].wait()

    def chunk(q):
        part[q] = residue(GRAD, q)

    def leaf(side, i):
        src, dst, device = (
            (part.at[place(z + 2 * steps - 1 - 2 * i)], right_leaf.at[i], up),
            (part.at[place(z - 2 * steps + 1 + 2 * i)], left_leaf.at[i], down),
        )[side]
        return hop(src, dst, leaf_send.at[side, i], leaf_recv.at[side, i], device)

    def chain(side, step, source):
        box, device = ((right_box, up_two), (left_box, down_two))[side]
        return [
            hop(source(c), box.at[step, c], sum_send.at[side, step, i], sum_recv.at[side, step, i], device)
            for i, c in enumerate(cuts)
        ]

    chunk(place(z + 2 * steps))
    right = chain(0, 0, lambda c: part.at[place(z + 2 * steps), c])
    chunk(place(z - 2 * steps + 1))
    left_leaves = [leaf(1, 0)]
    chunk(place(z + 2 * steps - 1))
    right_leaves = [leaf(0, 0)]

    def others(step, carry):
        chunk(place(z - 2 * steps + 1 + step))
        return carry

    lax.fori_loop(1, rings - 2, others, 0, unroll=rings - 3)
    for i in range(1, steps - 1):
        left_leaves.append(leaf(1, i))
        right_leaves.append(leaf(0, i))

    def sum_left(step, left):
        left_leaves[step].wait_recv()
        q = place(z - 2 * steps + 2 + 2 * step)
        if step == 0:
            for c in cuts:
                left_leaf[0, c] += part[q, c]
            return chain(1, 0, lambda c: left_leaf.at[0, c])
        for i, c in enumerate(cuts):
            left[i].wait_recv()
            left_box[step - 1, c] += part[q, c] + left_leaf[step, c]
        if step == steps - 2:
            return land(1, rings - 2, lambda c: left_box.at[step - 1, c])
        return chain(1, step, lambda c: left_box.at[step - 1, c])

    def sum_right(step, right):
        right_leaves[step - 1].wait_recv()
        q = place(z + 2 * steps - 2 * step)
        for i, c in enumerate(cuts):
            right[i].wait_recv()
            right_box[step - 1, c] += part[q, c] + right_leaf[step - 1, c]
        if step == steps - 1:
            return land(0, 2, lambda c: right_box.at[step - 1, c])
        return chain(0, step, lambda c: right_box.at[step - 1, c])

    half = rows // 2
    kept = pl.ds(pl.multiple_of(x * half, half), half)
    given = pl.ds(pl.multiple_of((1 - x) * half, half), half)

    def land(kind, move, source):
        for rail in range(2):
            device = {"dp": lax.rem(z + move, rings) * 2 + rail}
            hop(
                source(pl.ds(rail * half, half)), landing.at[kind, x],
                land_send.at[kind, rail], land_recv.at[kind, x], device,
            )

    def landed(kind, rail):
        pltpu.make_async_remote_copy(
            src_ref=landing.at[kind, rail], dst_ref=landing.at[kind, rail],
            send_sem=land_send.at[kind, rail], recv_sem=land_recv.at[kind, rail],
            device_id=twin, device_id_type=MESH,
        ).wait_recv()

    gift = hop(part.at[z, given], landing.at[4, 0], land_send.at[4, 0], land_recv.at[4, 0], twin)
    land(2, 1, lambda c: part.at[place(z + 1), c])
    land(3, rings - 1, lambda c: part.at[place(z - 1), c])
    send_in(DU)
    left = sum_left(0, None)
    right = sum_right(1, right)
    mix(U, H, U, False, True, False)
    finish(U)
    send_out(U)
    left = sum_left(1, left)
    right = sum_right(2, right)
    mix(G, H, G, True, True, False)
    finish(G)
    send_out(G)
    sum_left(2, left)
    sum_right(3, right)
    receive(DU)
    load(DU)
    analyse(DU, (DU,))
    mix(DU, H, DU, False, False, False)
    gift.wait_recv()
    mine_sum = part[z, kept] + landing[4, 0]
    for kind in (2, 3, 1, 0):
        for rail in range(2):
            landed(kind, rail)
        mine_sum = mine_sum + (landing[kind, 0] + landing[kind, 1])
    total[z, kept] = mine_sum

    shared = []

    def spread(side, step, last_chain):
        index = place(z - 2 * step) if side == 0 else place(z + 2 * step)
        two, one = ((up_two, up), (down_two, down))[side]
        here = total.at[index, kept]
        first = None
        if not last_chain:
            first = hop(here, here, all_send.at[side, step], all_recv.at[side, step], two)
        second = hop(here, here, near_send.at[side, step], near_recv.at[side, step], one)
        if side == 0 or step:
            share(index)
        return first, second

    def share(index):
        here = total.at[index, kept]
        i = len(shared)
        shared.append(hop(here, here, twin_send.at[i], twin_recv.at[i], twin))

    right, right_near = spread(0, 0, False)
    left, left_near = spread(1, 0, False)
    finish(DU)
    send_out(DU)
    for step in range(1, steps):
        behind = (right_near, left_near)
        right.wait_recv()
        right, right_near = spread(0, step, False)
        left.wait_recv()
        left, left_near = spread(1, step, step == steps - 1)
        behind[0].wait_recv()
        share(place(z - 2 * step + 1))
        behind[1].wait_recv()
        share(place(z + 2 * step - 1))
    right.wait_recv()
    share(place(z - 2 * steps))
    right_near.wait_recv()
    share(place(z - 2 * steps + 1))
    left_near.wait_recv()
    share(place(z + 2 * steps - 1))
    for copy in shared:
        copy.wait_recv()
    for q in range(SPLIT):
        grad_ref[pl.ds(q, rows, stride=SPLIT), :] = total[q] * scale
    for copy in started + sent:
        copy.wait_send()
    for copy in finished:
        copy.wait()


def fused(u, g, du, h, tables, scale):
    n = lax.axis_size("ctx")
    rings = lax.axis_size("dp") // 2
    length, width = h.shape
    rows = length // SPLIT
    steps = rings // 4
    anywhere = pl.BlockSpec(memory_space=pl.ANY)
    whole = pl.BlockSpec(memory_space=pltpu.VMEM)
    shape = jax.ShapeDtypeStruct((1, length // n, n * width), jnp.bfloat16)
    sem = pltpu.SemaphoreType.DMA

    def space(*sizes, kind=jnp.float32):
        return pltpu.VMEM(sizes, kind)

    half = jnp.bfloat16
    return pl.pallas_call(
        functools.partial(fused_kernel, n, rings, scale),
        out_shape=(shape,) * 3 + (jax.ShapeDtypeStruct((length, width), jnp.float32),),
        in_specs=[anywhere] * 6 + [whole] * 2,
        out_specs=(anywhere,) * 3 + (whole,),
        scratch_shapes=[
            space(3, length, width, kind=half),
            space(3, length, width, kind=half),
            space(length, width),
            space(*tables[0].shape, kind=half),
            space(*tables[1].shape, kind=half),
            space(3, length, width),
            space(4, SPLIT, 2 * rows, width),
            space(4, SPLIT, 2 * rows, width),
            space(2 * SPLIT, width),
            space(4, 2 * SPLIT, width),
            space(2 * SPLIT, width),
            space(4, 2 * SPLIT, width),
            space(rings, rows, width),
            space(steps - 1, rows, width),
            space(steps - 1, rows, width),
            space(steps - 1, rows, width),
            space(steps - 1, rows, width),
            space(5, 2, rows // 2, width),
            space(rings, rows, width),
            sem((3,)), sem((6,)),
            sem((3, n)), sem((3, n)), sem((3, n)), sem((3, n)),
            sem((2, steps, SUBS)), sem((2, steps, SUBS)), sem((2, steps)), sem((2, steps)), sem((5, 2)), sem((5, 2)),
            sem((2, steps)), sem((2, steps)), sem((2, steps)), sem((2, steps)), sem((rings,)), sem((rings,)),
        ],
        compiler_params=pltpu.CompilerParams(
            collective_id=0, has_side_effects=True, vmem_limit_bytes=60 * MIB
        ),
        name="hyena",
    )(u, g, du, h, *tables)


def copy_kernel(count, *refs):
    sources, targets, staged = refs[:count], refs[count : 2 * count], refs[2 * count : 3 * count]
    read_sem, write_sem = refs[3 * count :]
    reads = [pltpu.make_async_copy(sources[i], staged[i], read_sem.at[i]) for i in range(count)]
    writes = [pltpu.make_async_copy(staged[i], targets[i], write_sem.at[i]) for i in range(count)]
    for copy in reads:
        copy.start()
    for i in range(count):
        reads[i].wait()
        writes[i].start()
    for copy in writes:
        copy.wait()


def copied(*arrays):
    count = len(arrays)
    anywhere = pl.BlockSpec(memory_space=pl.ANY)
    return pl.pallas_call(
        functools.partial(copy_kernel, count),
        out_shape=tuple(jax.ShapeDtypeStruct(a.shape, a.dtype) for a in arrays),
        in_specs=[anywhere] * count,
        out_specs=(anywhere,) * count,
        scratch_shapes=[pltpu.VMEM(a.shape, a.dtype) for a in arrays]
        + [pltpu.SemaphoreType.DMA((count,)), pltpu.SemaphoreType.DMA((count,))],
        compiler_params=pltpu.CompilerParams(vmem_limit_bytes=60 * MIB),
        name="results",
    )(*arrays)


def local(primal, tangent, cotangent, impulse):
    length = impulse.shape[0]
    tables = [jnp.asarray(t) for t in build_tables(length)]
    scale = 1.0 / math.sqrt(lax.axis_size("dp") * length)
    back_u, back_g, back_du, summed = copied(*fused(primal, cotangent, tangent, impulse, tables, scale))
    return (back_u, back_du, back_g, summed)


def solution(mesh):
    placed = (P("dp", "ctx", None), P("dp", "ctx", None), P("dp", "ctx", None), P(None, "ctx"))
    return jax.shard_map(
        local,
        mesh=mesh,
        in_specs=placed,
        out_specs=(
            P("dp", "ctx", None),
            P("dp", "ctx", None),
            P("dp", "ctx", None),
            P(None, "ctx"),
        ),
        check_vma=False,
    )
```

```python
import functools
import math

import jax
import jax.numpy as jnp
import ml_dtypes
import numpy as np
from jax import lax
from jax.experimental import pallas as pl
from jax.experimental.pallas import tpu as pltpu
from jax.sharding import PartitionSpec as P

MESH = pl.DeviceIdType.MESH
LANES = 128
SPLIT = 16
MIB = 1024 * 1024
UNROLL = 16


def two_pieces(table):
    high = table.astype(ml_dtypes.bfloat16)
    low = (table - high.astype(np.float64)).astype(ml_dtypes.bfloat16)
    return high, low


def build_tables(length):
    total = 2 * length
    rows = length // SPLIT
    time = np.arange(rows)[None, :] * SPLIT + np.arange(SPLIT)[:, None]
    angle = 2.0 * np.pi * (time[:, None, :] * np.arange(rows)[None, :, None] % total) / total
    real, imag = np.cos(angle), -np.sin(angle)
    real[:, 0, :] = 1.0
    imag[:, 0, :] = 1.0 - 2.0 * (np.arange(rows) % 2)
    high, low = two_pieces(np.concatenate([real, imag], 1))
    analysis = np.concatenate([high, low], 2)
    real, imag = np.cos(angle) * (2.0 / total), -np.sin(angle) * (2.0 / total)
    real[:, 0, :] = (np.arange(rows) % 2 == 0)[None, :]
    imag[:, 0, :] = (np.arange(rows) % 2 == 1)[None, :]
    high, low = two_pieces(np.concatenate([real, imag], 1).transpose(0, 2, 1))
    synthesis = np.concatenate([high, low], 1)
    edge = np.zeros((2 * SPLIT, 2 * SPLIT))
    back = np.zeros((2 * SPLIT, 2 * SPLIT))
    point = np.arange(SPLIT)
    folded = np.arange(2 * SPLIT)
    for m in range(SPLIT):
        turn = 2.0 * np.pi * m * point / (2 * SPLIT)
        start = SPLIT * (m % 2)
        edge[m, start : start + SPLIT] = np.cos(turn)
        full = 2.0 * np.pi * m * folded / (2 * SPLIT)
        if m:
            edge[SPLIT + m, start : start + SPLIT] = -np.sin(turn)
            back[:, m] = 2.0 * np.cos(full) / total
            back[:, SPLIT + m] = -2.0 * np.sin(full) / total
    edge[SPLIT, :SPLIT] = np.cos(np.pi * point)
    back[:, 0] = 1.0 / total
    back[:, SPLIT] = np.cos(np.pi * folded) / total
    return analysis, synthesis, edge.astype(np.float32), back.astype(np.float32)


def times(value, power, sign):
    re, im = value
    power = (power * sign) % 16
    if power == 0:
        return (re, im)
    if power == 4:
        return (-im, re)
    if power == 8:
        return (-re, -im)
    if power == 12:
        return (im, -re)
    c, s = math.cos(math.pi * power / 8), math.sin(math.pi * power / 8)
    if power % 4 == 2:
        size = math.sqrt(0.5)
        if power == 2:
            return ((re - im) * size, (re + im) * size)
        if power == 6:
            return ((re + im) * -size, (re - im) * size)
        if power == 10:
            return ((im - re) * size, (re + im) * -size)
        return ((re + im) * size, (im - re) * size)
    return (re * c - im * s, re * s + im * c)


def four(a, b, c, d, sign):
    sr, si = a[0] + c[0], a[1] + c[1]
    dr, di = a[0] - c[0], a[1] - c[1]
    tr, ti = b[0] + d[0], b[1] + d[1]
    er, ei = b[0] - d[0], b[1] - d[1]
    plus = (dr - ei, di + er)
    minus = (dr + ei, di - er)
    if sign < 0:
        plus, minus = minus, plus
    return ((sr + tr, si + ti), plus, (sr - tr, si - ti), minus)


def sixteen(points, sign):
    inner = [four(points[b], points[4 + b], points[8 + b], points[12 + b], sign) for b in range(4)]
    result = [None] * 16
    for c in range(4):
        column = [times(inner[b][c], b * c, sign) for b in range(4)]
        outer = four(*column, sign)
        for d in range(4):
            result[c + 4 * d] = outer[d]
    return result


def product(a, b, conjugate):
    if conjugate:
        return (a[0] * b[0] + a[1] * b[1], a[0] * b[1] - a[1] * b[0])
    return (a[0] * b[0] - a[1] * b[1], a[0] * b[1] + a[1] * b[0])


U, G, DU, H = range(4)
GRAD = 3
SUBS = 2


def encode(total, index, piece, value):
    top = jnp.max(jnp.abs(value), axis=0, keepdims=True).astype(jnp.bfloat16)
    size = top.astype(jnp.float32)
    scaled = value * jnp.where(size > 0.0, 1.0 / size, 0.0)
    fourth = (scaled * scaled) * (scaled * scaled) * 2.0**60
    code = fourth * fourth
    code = jnp.where(scaled < 0.0, -code, code)
    total[index, piece, : value.shape[0]] = code.astype(jnp.bfloat16)
    total[index, piece, value.shape[0] :] = jnp.broadcast_to(top, (16, top.shape[1]))


def decoded(total, index, piece):
    rows = total.shape[2] - 16
    code = total[index, piece, :rows].astype(jnp.float32)
    size = total[index, piece, rows:].astype(jnp.float32)[0:1]
    root = jnp.sqrt(jnp.sqrt(jnp.sqrt(jnp.abs(code)) * 2.0**-60))
    return jnp.where(code < 0.0, -root, root) * size


def fused_kernel(
    n, rings, scale,
    u_ref, g_ref, du_ref, h_ref, analysis_ref, synthesis_ref, edge, back,
    ou_ref, og_ref, odu_ref, grad_ref,
    arrive, leave, impulse, analysis, synthesis, signal, spec, prod, rim, rim_spec, rim_mix, rim_out,
    part, right_box, left_box, right_leaf, left_leaf, landing, total,
    table_sem, local_sem, in_send, in_recv, out_send, out_recv, sum_send, sum_recv, leaf_send, leaf_recv, land_send, land_recv,
    all_send, all_recv, near_send, near_recv, twin_sem,
):
    me, dp = lax.axis_index("ctx"), lax.axis_index("dp")
    z, x = lax.div(dp, 2), lax.rem(dp, 2)
    up, up_two, down, down_two = (
        {"dp": lax.rem(z + move, rings) * 2 + x} for move in (1, 2, rings - 1, rings - 2)
    )
    twin = {"dp": z * 2 + 1 - x}
    around = [
        {"dp": lax.rem(z + move, rings) * 2 + 1 - x} for move in (1, 2, rings - 1, rings - 2)
    ]
    length = impulse.shape[0]
    rows = length // SPLIT
    tokens = length // n
    steps = rings // 4
    sub = rows // SUBS
    mine = pl.ds(pl.multiple_of(me * tokens, tokens), tokens)
    own = pl.ds(pl.multiple_of(me * LANES, LANES), LANES)

    tables = [
        pltpu.make_async_copy(src, dst, table_sem.at[i])
        for i, (src, dst) in enumerate(((h_ref, impulse), (analysis_ref, analysis), (synthesis_ref, synthesis)))
    ]
    for copy in tables:
        copy.start()
    barrier = pltpu.get_barrier_semaphore()
    for step in range(1, n):
        pl.semaphore_signal(
            barrier, inc=1, device_id={"ctx": lax.rem(me + step, n)}, device_id_type=MESH
        )
    for device in (up, up_two, down, down_two, twin, *around):
        pl.semaphore_signal(barrier, inc=1, device_id=device, device_id_type=MESH)
    pl.semaphore_wait(barrier, n + 8)

    remote, sent, locals_ = {}, [], {}

    def send_in(s):
        src = (u_ref, g_ref, du_ref)[s]
        remote[s] = []
        for step in range(1, n):
            other = lax.rem(me + step, n)
            copy = pltpu.make_async_remote_copy(
                src_ref=src.at[0, :, pl.ds(pl.multiple_of(other * LANES, LANES), LANES)],
                dst_ref=arrive.at[s, mine, :],
                send_sem=in_send.at[s, step], recv_sem=in_recv.at[s, step],
                device_id={"ctx": other}, device_id_type=MESH,
            )
            copy.start()
            remote[s].append(copy)
        locals_[s] = pltpu.make_async_copy(src.at[0, :, own], arrive.at[s, mine, :], local_sem.at[s])
        locals_[s].start()

    def receive(s):
        for copy in remote[s]:
            copy.wait_recv()
        locals_[s].wait()
        sent.extend(remote[s])

    finished = []

    def send_out(o):
        dst = (ou_ref, og_ref, odu_ref)[o]
        for step in range(1, n):
            other = lax.rem(me + step, n)
            copy = pltpu.make_async_remote_copy(
                src_ref=leave.at[o, pl.ds(pl.multiple_of(other * tokens, tokens), tokens), :],
                dst_ref=dst.at[0, :, own],
                send_sem=out_send.at[o, step], recv_sem=out_recv.at[o, step],
                device_id={"ctx": other}, device_id_type=MESH,
            )
            copy.start()
            finished.append(copy)
        copy = pltpu.make_async_copy(leave.at[o, mine, :], dst.at[0, :, own], local_sem.at[3 + o])
        copy.start()
        finished.append(copy)

    def analyse(s, slots):
        def body(q, carry):
            pieces = [signal[i, pl.ds(q, rows, stride=SPLIT), :].astype(jnp.bfloat16) for i in slots]
            block = jnp.concatenate(pieces, 1) if len(slots) > 1 else pieces[0]
            block = jnp.concatenate([block, block], 0)
            out = jnp.dot(analysis[q], block, preferred_element_type=jnp.float32)
            if len(slots) > 1:
                out = out[:, :LANES] + out[:, LANES:]
            spec[s, q] = out
            rim[pl.ds(q, 1), :] = out[0:1]
            rim[pl.ds(SPLIT + q, 1), :] = out[rows : rows + 1]
            return carry

        lax.fori_loop(0, SPLIT, body, 0, unroll=UNROLL)
        rim_spec[s] = jnp.dot(
            edge[...], rim[...], precision=lax.Precision.HIGHEST, preferred_element_type=jnp.float32
        )

    def mix(o, a, b, conjugate, turned, kept):
        left, right = (rim_spec[a, :SPLIT], rim_spec[a, SPLIT:]), (rim_spec[b, :SPLIT], rim_spec[b, SPLIT:])
        re, im = product(left, right, conjugate)
        first = lax.broadcasted_iota(jnp.int32, (SPLIT, LANES), 0) == 0
        rim_mix[:SPLIT] = jnp.where(first, left[0] * right[0], re)
        rim_mix[SPLIT:] = jnp.where(first, left[1] * right[1], im)
        rim_out[o] = jnp.dot(
            back[...], rim_mix[...], precision=lax.Precision.HIGHEST, preferred_element_type=jnp.float32
        )

        def body(tile, carry):
            upper = pl.ds(pl.multiple_of(tile * 8, 8), 8)
            lower = pl.ds(pl.multiple_of(rows + tile * 8, 8), 8)
            points = [(spec[b, j, upper, :], spec[b, j, lower, :]) for j in range(SPLIT)]
            if not turned:
                points = sixteen(points, -1)
                if kept:
                    for j in range(SPLIT):
                        spec[b, j, upper, :] = points[j][0]
                        spec[b, j, lower, :] = points[j][1]
            points = [
                product((spec[a, j, upper, :], spec[a, j, lower, :]), points[j], conjugate)
                for j in range(SPLIT)
            ]
            points = sixteen(points, 1)
            for q in range(SPLIT):
                prod[o, q, upper, :] = points[q][0]
                prod[o, q, lower, :] = points[q][1]
            return carry

        lax.fori_loop(0, rows // 8, body, 0)

    def turn(s):
        def body(tile, carry):
            upper = pl.ds(pl.multiple_of(tile * 8, 8), 8)
            lower = pl.ds(pl.multiple_of(rows + tile * 8, 8), 8)
            points = sixteen([(spec[s, q, upper, :], spec[s, q, lower, :]) for q in range(SPLIT)], -1)
            for j in range(SPLIT):
                spec[s, j, upper, :] = points[j][0]
                spec[s, j, lower, :] = points[j][1]
            return carry

        lax.fori_loop(0, rows // 8, body, 0)

    def residue(o, q):
        prod[o, q, 0:1, :] = rim_out[o, pl.ds(q, 1), :]
        prod[o, q, rows : rows + 1, :] = rim_out[o, pl.ds(SPLIT + q, 1), :]
        block = prod[o, q]
        top = block.astype(jnp.bfloat16)
        rest = (block - top.astype(jnp.float32)).astype(jnp.bfloat16)
        both = jnp.dot(synthesis[q], top, preferred_element_type=jnp.float32)
        more = jnp.dot(synthesis[q, :rows], rest, preferred_element_type=jnp.float32)
        return both[:rows] + (both[rows:] + more)

    def finish(o):
        def body(q, carry):
            signal[o, pl.ds(q, rows, stride=SPLIT), :] = residue(o, q)
            return carry

        lax.fori_loop(0, SPLIT, body, 0, unroll=UNROLL)
        leave[o] = signal[o].astype(jnp.bfloat16)

    def load(s):
        signal[s] = arrive[s].astype(jnp.float32)

    def place(index):
        return lax.rem(index + 2 * rings, rings)

    started = []

    def hop(src, dst, sends, recvs, device):
        copy = pltpu.make_async_remote_copy(
            src_ref=src, dst_ref=dst, send_sem=sends, recv_sem=recvs, device_id=device, device_id_type=MESH
        )
        copy.start()
        started.append(copy)
        return copy

    cuts = [pl.ds(c * sub, sub) for c in range(SUBS)]

    send_in(U)
    send_in(G)
    tables[0].wait()
    high = impulse[...].astype(jnp.bfloat16).astype(jnp.float32)
    signal[0] = high
    signal[1] = impulse[...] - high
    tables[1].wait()
    analyse(H, (0, 1))
    turn(H)
    receive(U)
    load(U)
    analyse(U, (U,))
    turn(U)
    receive(G)
    load(G)
    analyse(G, (G,))
    mix(GRAD, U, G, True, False, True)
    tables[2].wait()

    def chunk(q):
        part[q] = residue(GRAD, q)

    def leaf(side, i):
        src, dst, device = (
            (part.at[place(z + 2 * steps - 1 - 2 * i)], right_leaf.at[i], up),
            (part.at[place(z - 2 * steps + 1 + 2 * i)], left_leaf.at[i], down),
        )[side]
        return hop(src, dst, leaf_send.at[side, i], leaf_recv.at[side, i], device)

    def chain(side, step, source):
        box, device = ((right_box, up_two), (left_box, down_two))[side]
        return [
            hop(source(c), box.at[step, c], sum_send.at[side, step, i], sum_recv.at[side, step, i], device)
            for i, c in enumerate(cuts)
        ]

    chunk(place(z + 2 * steps))
    right = chain(0, 0, lambda c: part.at[place(z + 2 * steps), c])
    chunk(place(z - 2 * steps + 1))
    left_leaves = [leaf(1, 0)]
    chunk(place(z + 2 * steps - 1))
    right_leaves = [leaf(0, 0)]

    def others(step, carry):
        chunk(place(z - 2 * steps + 1 + step))
        return carry

    lax.fori_loop(1, rings - 2, others, 0, unroll=rings - 3)
    for i in range(1, steps - 1):
        left_leaves.append(leaf(1, i))
        right_leaves.append(leaf(0, i))

    def sum_left(step, left):
        left_leaves[step].wait_recv()
        q = place(z - 2 * steps + 2 + 2 * step)
        if step == 0:
            for c in cuts:
                left_leaf[0, c] += part[q, c]
            return chain(1, 0, lambda c: left_leaf.at[0, c])
        for i, c in enumerate(cuts):
            left[i].wait_recv()
            left_box[step - 1, c] += part[q, c] + left_leaf[step, c]
        if step == steps - 2:
            return land(1, rings - 2, lambda c: left_box.at[step - 1, c])
        return chain(1, step, lambda c: left_box.at[step - 1, c])

    def sum_right(step, right):
        right_leaves[step - 1].wait_recv()
        q = place(z + 2 * steps - 2 * step)
        for i, c in enumerate(cuts):
            right[i].wait_recv()
            right_box[step - 1, c] += part[q, c] + right_leaf[step - 1, c]
        if step == steps - 1:
            return land(0, 2, lambda c: right_box.at[step - 1, c])
        return chain(0, step, lambda c: right_box.at[step - 1, c])

    half = rows // 2
    kept = pl.ds(pl.multiple_of(x * half, half), half)
    given = pl.ds(pl.multiple_of((1 - x) * half, half), half)

    def land(kind, move, source):
        for rail in range(2):
            device = {"dp": lax.rem(z + move, rings) * 2 + rail}
            hop(
                source(pl.ds(rail * half, half)), landing.at[kind, x],
                land_send.at[kind, rail], land_recv.at[kind, x], device,
            )

    def landed(kind, rail):
        pltpu.make_async_remote_copy(
            src_ref=landing.at[kind, rail], dst_ref=landing.at[kind, rail],
            send_sem=land_send.at[kind, rail], recv_sem=land_recv.at[kind, rail],
            device_id=twin, device_id_type=MESH,
        ).wait_recv()

    gift = hop(part.at[z, given], landing.at[4, 0], land_send.at[4, 0], land_recv.at[4, 0], twin)
    land(2, 1, lambda c: part.at[place(z + 1), c])
    land(3, rings - 1, lambda c: part.at[place(z - 1), c])
    send_in(DU)
    left = sum_left(0, None)
    right = sum_right(1, right)
    mix(U, H, U, False, True, False)
    finish(U)
    send_out(U)
    left = sum_left(1, left)
    right = sum_right(2, right)
    mix(G, H, G, True, True, False)
    finish(G)
    send_out(G)
    sum_left(2, left)
    sum_right(3, right)
    receive(DU)
    load(DU)
    analyse(DU, (DU,))
    mix(DU, H, DU, False, False, False)
    gift.wait_recv()
    mine_sum = part[z, kept] + landing[4, 0]
    for kind in (2, 3, 1, 0):
        for rail in range(2):
            landed(kind, rail)
        mine_sum = mine_sum + (landing[kind, 0] + landing[kind, 1])
    encode(total, z, x, mine_sum)

    streams = (x, 1 - x)

    def spread(side, step, i, last_chain):
        index = place(z - 2 * step) if side == 0 else place(z + 2 * step)
        two, one = ((up_two, up), (down_two, down))[side]
        here = total.at[index, streams[i]]
        first = None
        if not last_chain:
            first = hop(here, here, all_send.at[side, step, i], all_recv.at[side, step, i], two)
        return first, hop(here, here, near_send.at[side, step, i], near_recv.at[side, step, i], one)

    def decode(q):
        for part_of in range(2):
            grad_ref[pl.ds(q + part_of * half * SPLIT, half, stride=SPLIT), :] = decoded(total, q, part_of) * scale

    here = total.at[z, x]
    swap = hop(here, here, twin_sem.at[0], twin_sem.at[1], twin)
    far, near = {}, {}
    for i in range(2):
        if i:
            swap.wait_recv()
        for side in range(2):
            far[side, i], near[side, i] = spread(side, 0, i, False)
    finish(DU)
    send_out(DU)
    decode(z)
    for step in range(1, steps):
        behind = dict(near)
        for i in range(2):
            for side in range(2):
                far[side, i].wait_recv()
                far[side, i], near[side, i] = spread(side, step, i, side == 1 and step == steps - 1)
        decode(place(z - 2 * step))
        decode(place(z + 2 * step))
        for side in range(2):
            for i in range(2):
                behind[side, i].wait_recv()
            decode(place(z - 2 * step + 1) if side == 0 else place(z + 2 * step - 1))
    for i in range(2):
        far[0, i].wait_recv()
    decode(place(z - 2 * steps))
    for side in range(2):
        for i in range(2):
            near[side, i].wait_recv()
        decode(place(z - 2 * steps + 1) if side == 0 else place(z + 2 * steps - 1))
    for copy in started + sent:
        copy.wait_send()
    for copy in finished:
        copy.wait()


def fused(u, g, du, h, tables, scale):
    n = lax.axis_size("ctx")
    rings = lax.axis_size("dp") // 2
    length, width = h.shape
    rows = length // SPLIT
    steps = rings // 4
    anywhere = pl.BlockSpec(memory_space=pl.ANY)
    whole = pl.BlockSpec(memory_space=pltpu.VMEM)
    shape = jax.ShapeDtypeStruct((1, length // n, n * width), jnp.bfloat16)
    sem = pltpu.SemaphoreType.DMA

    def space(*sizes, kind=jnp.float32):
        return pltpu.VMEM(sizes, kind)

    half = jnp.bfloat16
    return pl.pallas_call(
        functools.partial(fused_kernel, n, rings, scale),
        out_shape=(shape,) * 3 + (jax.ShapeDtypeStruct((length, width), jnp.float32),),
        in_specs=[anywhere] * 6 + [whole] * 2,
        out_specs=(anywhere,) * 3 + (whole,),
        scratch_shapes=[
            space(3, length, width, kind=half),
            space(3, length, width, kind=half),
            space(length, width),
            space(*tables[0].shape, kind=half),
            space(*tables[1].shape, kind=half),
            space(3, length, width),
            space(4, SPLIT, 2 * rows, width),
            space(4, SPLIT, 2 * rows, width),
            space(2 * SPLIT, width),
            space(4, 2 * SPLIT, width),
            space(2 * SPLIT, width),
            space(4, 2 * SPLIT, width),
            space(rings, rows, width),
            space(steps - 1, rows, width),
            space(steps - 1, rows, width),
            space(steps - 1, rows, width),
            space(steps - 1, rows, width),
            space(5, 2, rows // 2, width),
            space(rings, 2, rows // 2 + 16, width, kind=half),
            sem((3,)), sem((6,)),
            sem((3, n)), sem((3, n)), sem((3, n)), sem((3, n)),
            sem((2, steps, SUBS)), sem((2, steps, SUBS)), sem((2, steps)), sem((2, steps)), sem((5, 2)), sem((5, 2)),
            sem((2, steps, 2)), sem((2, steps, 2)), sem((2, steps, 2)), sem((2, steps, 2)), sem((2,)),
        ],
        compiler_params=pltpu.CompilerParams(
            collective_id=0, has_side_effects=True, vmem_limit_bytes=60 * MIB
        ),
        name="hyena",
    )(u, g, du, h, *tables)


def copy_kernel(count, *refs):
    sources, targets, staged = refs[:count], refs[count : 2 * count], refs[2 * count : 3 * count]
    read_sem, write_sem = refs[3 * count :]
    reads, writes = [], []
    for i in range(count):
        for piece in range(2):
            size = sources[i].shape[-2] // 2
            cut = (0,) * (len(sources[i].shape) - 2) + (pl.ds(piece * size, size),)
            source, middle, target = sources[i].at[cut], staged[i].at[cut], targets[i].at[cut]
            reads.append(pltpu.make_async_copy(source, middle, read_sem.at[i, piece]))
            writes.append(pltpu.make_async_copy(middle, target, write_sem.at[i, piece]))
    for copy in reads:
        copy.start()
    for read, write in zip(reads, writes):
        read.wait()
        write.start()
    for copy in writes:
        copy.wait()


def copied(*arrays):
    count = len(arrays)
    anywhere = pl.BlockSpec(memory_space=pl.ANY)
    return pl.pallas_call(
        functools.partial(copy_kernel, count),
        out_shape=tuple(jax.ShapeDtypeStruct(a.shape, a.dtype) for a in arrays),
        in_specs=[anywhere] * count,
        out_specs=(anywhere,) * count,
        scratch_shapes=[pltpu.VMEM(a.shape, a.dtype) for a in arrays]
        + [pltpu.SemaphoreType.DMA((count, 2)), pltpu.SemaphoreType.DMA((count, 2))],
        compiler_params=pltpu.CompilerParams(vmem_limit_bytes=60 * MIB),
        name="results",
    )(*arrays)


def local(primal, tangent, cotangent, impulse):
    length = impulse.shape[0]
    tables = [jnp.asarray(t) for t in build_tables(length)]
    scale = 1.0 / math.sqrt(lax.axis_size("dp") * length)
    back_u, back_g, back_du, summed = copied(*fused(primal, cotangent, tangent, impulse, tables, scale))
    return (back_u, back_du, back_g, summed)


def solution(mesh):
    placed = (P("dp", "ctx", None), P("dp", "ctx", None), P("dp", "ctx", None), P(None, "ctx"))
    return jax.shard_map(
        local,
        mesh=mesh,
        in_specs=placed,
        out_specs=(
            P("dp", "ctx", None),
            P("dp", "ctx", None),
            P("dp", "ctx", None),
            P(None, "ctx"),
        ),
        check_vma=False,
    )
```

```python
import functools
import math

import jax
import jax.numpy as jnp
import ml_dtypes
import numpy as np
from jax import lax
from jax.experimental import pallas as pl
from jax.experimental.pallas import tpu as pltpu
from jax.sharding import PartitionSpec as P

MESH = pl.DeviceIdType.MESH
LANES = 128
SPLIT = 16
MIB = 1024 * 1024
UNROLL = 16


def two_pieces(table):
    high = table.astype(ml_dtypes.bfloat16)
    low = (table - high.astype(np.float64)).astype(ml_dtypes.bfloat16)
    return high, low


def build_tables(length):
    total = 2 * length
    rows = length // SPLIT
    time = np.arange(rows)[None, :] * SPLIT + np.arange(SPLIT)[:, None]
    angle = 2.0 * np.pi * (time[:, None, :] * np.arange(rows)[None, :, None] % total) / total
    real, imag = np.cos(angle), -np.sin(angle)
    real[:, 0, :] = 1.0
    imag[:, 0, :] = 1.0 - 2.0 * (np.arange(rows) % 2)
    high, low = two_pieces(np.concatenate([real, imag], 1))
    analysis = np.concatenate([high, low], 2)
    real, imag = np.cos(angle) * (2.0 / total), -np.sin(angle) * (2.0 / total)
    real[:, 0, :] = (np.arange(rows) % 2 == 0)[None, :]
    imag[:, 0, :] = (np.arange(rows) % 2 == 1)[None, :]
    high, low = two_pieces(np.concatenate([real, imag], 1).transpose(0, 2, 1))
    synthesis = np.concatenate([high, low], 1)
    edge = np.zeros((2 * SPLIT, 2 * SPLIT))
    back = np.zeros((2 * SPLIT, 2 * SPLIT))
    point = np.arange(SPLIT)
    folded = np.arange(2 * SPLIT)
    for m in range(SPLIT):
        turn = 2.0 * np.pi * m * point / (2 * SPLIT)
        start = SPLIT * (m % 2)
        edge[m, start : start + SPLIT] = np.cos(turn)
        full = 2.0 * np.pi * m * folded / (2 * SPLIT)
        if m:
            edge[SPLIT + m, start : start + SPLIT] = -np.sin(turn)
            back[:, m] = 2.0 * np.cos(full) / total
            back[:, SPLIT + m] = -2.0 * np.sin(full) / total
    edge[SPLIT, :SPLIT] = np.cos(np.pi * point)
    back[:, 0] = 1.0 / total
    back[:, SPLIT] = np.cos(np.pi * folded) / total
    return analysis, synthesis, edge.astype(np.float32), back.astype(np.float32)


def times(value, power, sign):
    re, im = value
    power = (power * sign) % 16
    if power == 0:
        return (re, im)
    if power == 4:
        return (-im, re)
    if power == 8:
        return (-re, -im)
    if power == 12:
        return (im, -re)
    c, s = math.cos(math.pi * power / 8), math.sin(math.pi * power / 8)
    if power % 4 == 2:
        size = math.sqrt(0.5)
        if power == 2:
            return ((re - im) * size, (re + im) * size)
        if power == 6:
            return ((re + im) * -size, (re - im) * size)
        if power == 10:
            return ((im - re) * size, (re + im) * -size)
        return ((re + im) * size, (im - re) * size)
    return (re * c - im * s, re * s + im * c)


def four(a, b, c, d, sign):
    sr, si = a[0] + c[0], a[1] + c[1]
    dr, di = a[0] - c[0], a[1] - c[1]
    tr, ti = b[0] + d[0], b[1] + d[1]
    er, ei = b[0] - d[0], b[1] - d[1]
    plus = (dr - ei, di + er)
    minus = (dr + ei, di - er)
    if sign < 0:
        plus, minus = minus, plus
    return ((sr + tr, si + ti), plus, (sr - tr, si - ti), minus)


def sixteen(points, sign):
    inner = [four(points[b], points[4 + b], points[8 + b], points[12 + b], sign) for b in range(4)]
    result = [None] * 16
    for c in range(4):
        column = [times(inner[b][c], b * c, sign) for b in range(4)]
        outer = four(*column, sign)
        for d in range(4):
            result[c + 4 * d] = outer[d]
    return result


def product(a, b, conjugate):
    if conjugate:
        return (a[0] * b[0] + a[1] * b[1], a[0] * b[1] - a[1] * b[0])
    return (a[0] * b[0] - a[1] * b[1], a[0] * b[1] + a[1] * b[0])


U, G, DU, H = range(4)
GRAD = 3
SUBS = 2


def encode(total, index, piece, value):
    top = jnp.max(jnp.abs(value), axis=0, keepdims=True).astype(jnp.bfloat16)
    size = top.astype(jnp.float32)
    scaled = value * jnp.where(size > 0.0, 1.0 / size, 0.0)
    fourth = (scaled * scaled) * (scaled * scaled) * 2.0**60
    code = fourth * fourth
    code = jnp.where(scaled < 0.0, -code, code)
    total[index, piece, : value.shape[0]] = code.astype(jnp.bfloat16)
    total[index, piece, value.shape[0] :] = jnp.broadcast_to(top, (16, top.shape[1]))


def decoded(total, index, piece):
    rows = total.shape[2] - 16
    code = total[index, piece, :rows].astype(jnp.float32)
    size = total[index, piece, rows:].astype(jnp.float32)[0:1]
    root = jnp.sqrt(jnp.sqrt(jnp.sqrt(jnp.abs(code)) * 2.0**-60))
    return jnp.where(code < 0.0, -root, root) * size


def fused_kernel(
    n, rings, scale,
    u_ref, g_ref, du_ref, h_ref, analysis_ref, synthesis_ref, edge, back,
    ou_ref, og_ref, odu_ref, grad_ref,
    arrive, leave, impulse, analysis, synthesis, signal, spec, prod, rim, rim_spec, rim_mix, rim_out,
    part, right_box, left_box, right_leaf, left_leaf, landing, total,
    table_sem, local_sem, in_send, in_recv, out_send, out_recv, sum_send, sum_recv, leaf_send, leaf_recv, land_send, land_recv,
    all_send, all_recv, near_send, near_recv, twin_sem,
):
    me, dp = lax.axis_index("ctx"), lax.axis_index("dp")
    z, x = lax.div(dp, 2), lax.rem(dp, 2)
    up, up_two, down, down_two = (
        {"dp": lax.rem(z + move, rings) * 2 + x} for move in (1, 2, rings - 1, rings - 2)
    )
    twin = {"dp": z * 2 + 1 - x}
    around = [
        {"dp": lax.rem(z + move, rings) * 2 + 1 - x} for move in (1, 2, rings - 1, rings - 2)
    ]
    length = impulse.shape[0]
    rows = length // SPLIT
    tokens = length // n
    steps = rings // 4
    sub = rows // SUBS
    mine = pl.ds(pl.multiple_of(me * tokens, tokens), tokens)
    own = pl.ds(pl.multiple_of(me * LANES, LANES), LANES)

    tables = [
        pltpu.make_async_copy(src, dst, table_sem.at[i])
        for i, (src, dst) in enumerate(((h_ref, impulse), (analysis_ref, analysis), (synthesis_ref, synthesis)))
    ]
    for copy in tables:
        copy.start()
    barrier = pltpu.get_barrier_semaphore()
    for step in range(1, n):
        pl.semaphore_signal(
            barrier, inc=1, device_id={"ctx": lax.rem(me + step, n)}, device_id_type=MESH
        )
    for device in (up, up_two, down, down_two, twin, *around):
        pl.semaphore_signal(barrier, inc=1, device_id=device, device_id_type=MESH)
    pl.semaphore_wait(barrier, n + 8)

    remote, sent, locals_ = {}, [], {}

    def send_in(s):
        src = (u_ref, g_ref, du_ref)[s]
        remote[s] = []
        for step in range(1, n):
            other = lax.rem(me + step, n)
            copy = pltpu.make_async_remote_copy(
                src_ref=src.at[0, :, pl.ds(pl.multiple_of(other * LANES, LANES), LANES)],
                dst_ref=arrive.at[s, mine, :],
                send_sem=in_send.at[s, step], recv_sem=in_recv.at[s, step],
                device_id={"ctx": other}, device_id_type=MESH,
            )
            copy.start()
            remote[s].append(copy)
        locals_[s] = pltpu.make_async_copy(src.at[0, :, own], arrive.at[s, mine, :], local_sem.at[s])
        locals_[s].start()

    def receive(s):
        for copy in remote[s]:
            copy.wait_recv()
        locals_[s].wait()
        sent.extend(remote[s])

    finished = []

    def send_out(o):
        dst = (ou_ref, og_ref, odu_ref)[o]
        for step in range(1, n):
            other = lax.rem(me + step, n)
            copy = pltpu.make_async_remote_copy(
                src_ref=leave.at[o, pl.ds(pl.multiple_of(other * tokens, tokens), tokens), :],
                dst_ref=dst.at[0, :, own],
                send_sem=out_send.at[o, step], recv_sem=out_recv.at[o, step],
                device_id={"ctx": other}, device_id_type=MESH,
            )
            copy.start()
            finished.append(copy)
        copy = pltpu.make_async_copy(leave.at[o, mine, :], dst.at[0, :, own], local_sem.at[3 + o])
        copy.start()
        finished.append(copy)

    def analyse(s, slots):
        def body(q, carry):
            pieces = [signal[i, pl.ds(q, rows, stride=SPLIT), :].astype(jnp.bfloat16) for i in slots]
            block = jnp.concatenate(pieces, 1) if len(slots) > 1 else pieces[0]
            block = jnp.concatenate([block, block], 0)
            out = jnp.dot(analysis[q], block, preferred_element_type=jnp.float32)
            if len(slots) > 1:
                out = out[:, :LANES] + out[:, LANES:]
            spec[s, q] = out
            rim[pl.ds(q, 1), :] = out[0:1]
            rim[pl.ds(SPLIT + q, 1), :] = out[rows : rows + 1]
            return carry

        lax.fori_loop(0, SPLIT, body, 0, unroll=UNROLL)
        rim_spec[s] = jnp.dot(
            edge[...], rim[...], precision=lax.Precision.HIGHEST, preferred_element_type=jnp.float32
        )

    def mix(o, a, b, conjugate, turned, kept):
        left, right = (rim_spec[a, :SPLIT], rim_spec[a, SPLIT:]), (rim_spec[b, :SPLIT], rim_spec[b, SPLIT:])
        re, im = product(left, right, conjugate)
        first = lax.broadcasted_iota(jnp.int32, (SPLIT, LANES), 0) == 0
        rim_mix[:SPLIT] = jnp.where(first, left[0] * right[0], re)
        rim_mix[SPLIT:] = jnp.where(first, left[1] * right[1], im)
        rim_out[o] = jnp.dot(
            back[...], rim_mix[...], precision=lax.Precision.HIGHEST, preferred_element_type=jnp.float32
        )

        def body(tile, carry):
            upper = pl.ds(pl.multiple_of(tile * 8, 8), 8)
            lower = pl.ds(pl.multiple_of(rows + tile * 8, 8), 8)
            points = [(spec[b, j, upper, :], spec[b, j, lower, :]) for j in range(SPLIT)]
            if not turned:
                points = sixteen(points, -1)
                if kept:
                    for j in range(SPLIT):
                        spec[b, j, upper, :] = points[j][0]
                        spec[b, j, lower, :] = points[j][1]
            points = [
                product((spec[a, j, upper, :], spec[a, j, lower, :]), points[j], conjugate)
                for j in range(SPLIT)
            ]
            points = sixteen(points, 1)
            for q in range(SPLIT):
                prod[o, q, upper, :] = points[q][0]
                prod[o, q, lower, :] = points[q][1]
            return carry

        lax.fori_loop(0, rows // 8, body, 0)

    def turn(s):
        def body(tile, carry):
            upper = pl.ds(pl.multiple_of(tile * 8, 8), 8)
            lower = pl.ds(pl.multiple_of(rows + tile * 8, 8), 8)
            points = sixteen([(spec[s, q, upper, :], spec[s, q, lower, :]) for q in range(SPLIT)], -1)
            for j in range(SPLIT):
                spec[s, j, upper, :] = points[j][0]
                spec[s, j, lower, :] = points[j][1]
            return carry

        lax.fori_loop(0, rows // 8, body, 0)

    def residue(o, q):
        prod[o, q, 0:1, :] = rim_out[o, pl.ds(q, 1), :]
        prod[o, q, rows : rows + 1, :] = rim_out[o, pl.ds(SPLIT + q, 1), :]
        block = prod[o, q]
        top = block.astype(jnp.bfloat16)
        rest = (block - top.astype(jnp.float32)).astype(jnp.bfloat16)
        both = jnp.dot(synthesis[q], top, preferred_element_type=jnp.float32)
        more = jnp.dot(synthesis[q, :rows], rest, preferred_element_type=jnp.float32)
        return both[:rows] + (both[rows:] + more)

    def finish(o):
        def body(q, carry):
            signal[o, pl.ds(q, rows, stride=SPLIT), :] = residue(o, q)
            return carry

        lax.fori_loop(0, SPLIT, body, 0, unroll=UNROLL)
        leave[o] = signal[o].astype(jnp.bfloat16)

    def load(s):
        signal[s] = arrive[s].astype(jnp.float32)

    def place(index):
        return lax.rem(index + 2 * rings, rings)

    started = []

    def hop(src, dst, sends, recvs, device):
        copy = pltpu.make_async_remote_copy(
            src_ref=src, dst_ref=dst, send_sem=sends, recv_sem=recvs, device_id=device, device_id_type=MESH
        )
        copy.start()
        started.append(copy)
        return copy

    cuts = [pl.ds(c * sub, sub) for c in range(SUBS)]

    send_in(U)
    send_in(G)
    tables[0].wait()
    high = impulse[...].astype(jnp.bfloat16).astype(jnp.float32)
    signal[0] = high
    signal[1] = impulse[...] - high
    tables[1].wait()
    analyse(H, (0, 1))
    turn(H)
    receive(U)
    load(U)
    analyse(U, (U,))
    turn(U)
    receive(G)
    load(G)
    analyse(G, (G,))
    mix(GRAD, U, G, True, False, True)
    tables[2].wait()

    def chunk(q):
        part[q] = residue(GRAD, q)

    def leaf(side, i):
        src, dst, device = (
            (part.at[place(z + 2 * steps - 1 - 2 * i)], right_leaf.at[i], up),
            (part.at[place(z - 2 * steps + 1 + 2 * i)], left_leaf.at[i], down),
        )[side]
        return hop(src, dst, leaf_send.at[side, i], leaf_recv.at[side, i], device)

    def chain(side, step, source):
        box, device = ((right_box, up_two), (left_box, down_two))[side]
        return [
            hop(source(c), box.at[step, c], sum_send.at[side, step, i], sum_recv.at[side, step, i], device)
            for i, c in enumerate(cuts)
        ]

    chunk(place(z + 2 * steps))
    right = chain(0, 0, lambda c: part.at[place(z + 2 * steps), c])
    chunk(place(z - 2 * steps + 1))
    left_leaves = [leaf(1, 0)]
    chunk(place(z + 2 * steps - 1))
    right_leaves = [leaf(0, 0)]

    def others(step, carry):
        chunk(place(z - 2 * steps + 1 + step))
        return carry

    lax.fori_loop(1, rings - 2, others, 0, unroll=rings - 3)
    left_leaves.append(leaf(1, 1))
    right_leaves.append(leaf(0, 1))

    def sum_left(step, left):
        left_leaves[step].wait_recv()
        q = place(z - 2 * steps + 2 + 2 * step)
        if step == 0:
            for c in cuts:
                left_leaf[0, c] += part[q, c]
            return chain(1, 0, lambda c: left_leaf.at[0, c])
        for i, c in enumerate(cuts):
            left[i].wait_recv()
            left_box[step - 1, c] += part[q, c] + left_leaf[step, c]
        if step == steps - 2:
            return land(1, rings - 2, lambda c: left_box.at[step - 1, c])
        return chain(1, step, lambda c: left_box.at[step - 1, c])

    def sum_right(step, right):
        right_leaves[step - 1].wait_recv()
        q = place(z + 2 * steps - 2 * step)
        for i, c in enumerate(cuts):
            right[i].wait_recv()
            right_box[step - 1, c] += part[q, c] + right_leaf[step - 1, c]
        if step == steps - 1:
            return land(0, 2, lambda c: right_box.at[step - 1, c])
        return chain(0, step, lambda c: right_box.at[step - 1, c])

    half = rows // 2
    kept = pl.ds(pl.multiple_of(x * half, half), half)
    given = pl.ds(pl.multiple_of((1 - x) * half, half), half)

    def land(kind, move, source):
        for rail in range(2):
            device = {"dp": lax.rem(z + move, rings) * 2 + rail}
            hop(
                source(pl.ds(rail * half, half)), landing.at[kind, x],
                land_send.at[kind, rail], land_recv.at[kind, x], device,
            )

    def landed(kind, rail):
        pltpu.make_async_remote_copy(
            src_ref=landing.at[kind, rail], dst_ref=landing.at[kind, rail],
            send_sem=land_send.at[kind, rail], recv_sem=land_recv.at[kind, rail],
            device_id=twin, device_id_type=MESH,
        ).wait_recv()

    send_in(DU)
    left = sum_left(0, None)
    right = sum_right(1, right)
    left_leaves.append(leaf(1, 2))
    right_leaves.append(leaf(0, 2))
    mix(U, H, U, False, True, False)
    finish(U)
    left = sum_left(1, left)
    right = sum_right(2, right)
    gift = hop(part.at[z, given], landing.at[4, 0], land_send.at[4, 0], land_recv.at[4, 0], twin)
    land(2, 1, lambda c: part.at[place(z + 1), c])
    land(3, rings - 1, lambda c: part.at[place(z - 1), c])
    send_out(U)
    mix(G, H, G, True, True, False)
    sum_left(2, left)
    sum_right(3, right)
    finish(G)
    receive(DU)
    load(DU)
    analyse(DU, (DU,))
    gift.wait_recv()
    mine_sum = part[z, kept] + landing[4, 0]
    for kind in (2, 3, 1, 0):
        for rail in range(2):
            landed(kind, rail)
        mine_sum = mine_sum + (landing[kind, 0] + landing[kind, 1])
    encode(total, z, x, mine_sum)

    streams = (x, 1 - x)

    def spread(side, step, i, last_chain):
        index = place(z - 2 * step) if side == 0 else place(z + 2 * step)
        two, one = ((up_two, up), (down_two, down))[side]
        here = total.at[index, streams[i]]
        first = None
        if not last_chain:
            first = hop(here, here, all_send.at[side, step, i], all_recv.at[side, step, i], two)
        return first, hop(here, here, near_send.at[side, step, i], near_recv.at[side, step, i], one)

    def decode(q):
        for part_of in range(2):
            grad_ref[pl.ds(q + part_of * half * SPLIT, half, stride=SPLIT), :] = decoded(total, q, part_of) * scale

    here = total.at[z, x]
    swap = hop(here, here, twin_sem.at[0], twin_sem.at[1], twin)
    far, near = {}, {}
    for i in range(2):
        if i:
            swap.wait_recv()
        for side in range(2):
            far[side, i], near[side, i] = spread(side, 0, i, False)
    send_out(G)
    mix(DU, H, DU, False, False, False)
    decode(z)
    for step in range(1, steps):
        behind = dict(near)
        for i in range(2):
            for side in range(2):
                far[side, i].wait_recv()
                far[side, i], near[side, i] = spread(side, step, i, side == 1 and step == steps - 1)
        if step == 1:
            finish(DU)
            send_out(DU)
        decode(place(z - 2 * step))
        decode(place(z + 2 * step))
        for side in range(2):
            for i in range(2):
                behind[side, i].wait_recv()
            decode(place(z - 2 * step + 1) if side == 0 else place(z + 2 * step - 1))
    for i in range(2):
        far[0, i].wait_recv()
    decode(place(z - 2 * steps))
    for side in range(2):
        for i in range(2):
            near[side, i].wait_recv()
        decode(place(z - 2 * steps + 1) if side == 0 else place(z + 2 * steps - 1))
    for copy in started + sent:
        copy.wait_send()
    for copy in finished:
        copy.wait()


def fused(u, g, du, h, tables, scale):
    n = lax.axis_size("ctx")
    rings = lax.axis_size("dp") // 2
    length, width = h.shape
    rows = length // SPLIT
    steps = rings // 4
    anywhere = pl.BlockSpec(memory_space=pl.ANY)
    whole = pl.BlockSpec(memory_space=pltpu.VMEM)
    shape = jax.ShapeDtypeStruct((1, length // n, n * width), jnp.bfloat16)
    sem = pltpu.SemaphoreType.DMA

    def space(*sizes, kind=jnp.float32):
        return pltpu.VMEM(sizes, kind)

    half = jnp.bfloat16
    return pl.pallas_call(
        functools.partial(fused_kernel, n, rings, scale),
        out_shape=(shape,) * 3 + (jax.ShapeDtypeStruct((length, width), jnp.float32),),
        in_specs=[anywhere] * 6 + [whole] * 2,
        out_specs=(anywhere,) * 3 + (whole,),
        scratch_shapes=[
            space(3, length, width, kind=half),
            space(3, length, width, kind=half),
            space(length, width),
            space(*tables[0].shape, kind=half),
            space(*tables[1].shape, kind=half),
            space(3, length, width),
            space(4, SPLIT, 2 * rows, width),
            space(4, SPLIT, 2 * rows, width),
            space(2 * SPLIT, width),
            space(4, 2 * SPLIT, width),
            space(2 * SPLIT, width),
            space(4, 2 * SPLIT, width),
            space(rings, rows, width),
            space(steps - 1, rows, width),
            space(steps - 1, rows, width),
            space(steps - 1, rows, width),
            space(steps - 1, rows, width),
            space(5, 2, rows // 2, width),
            space(rings, 2, rows // 2 + 16, width, kind=half),
            sem((3,)), sem((6,)),
            sem((3, n)), sem((3, n)), sem((3, n)), sem((3, n)),
            sem((2, steps, SUBS)), sem((2, steps, SUBS)), sem((2, steps)), sem((2, steps)), sem((5, 2)), sem((5, 2)),
            sem((2, steps, 2)), sem((2, steps, 2)), sem((2, steps, 2)), sem((2, steps, 2)), sem((2,)),
        ],
        compiler_params=pltpu.CompilerParams(
            collective_id=0, has_side_effects=True, vmem_limit_bytes=60 * MIB
        ),
        name="hyena",
    )(u, g, du, h, *tables)


def copy_kernel(count, *refs):
    sources, targets, staged = refs[:count], refs[count : 2 * count], refs[2 * count : 3 * count]
    read_sem, write_sem = refs[3 * count :]
    reads, writes = [], []
    for i in range(count):
        for piece in range(2):
            size = sources[i].shape[-2] // 2
            cut = (0,) * (len(sources[i].shape) - 2) + (pl.ds(piece * size, size),)
            source, middle, target = sources[i].at[cut], staged[i].at[cut], targets[i].at[cut]
            reads.append(pltpu.make_async_copy(source, middle, read_sem.at[i, piece]))
            writes.append(pltpu.make_async_copy(middle, target, write_sem.at[i, piece]))
    for copy in reads:
        copy.start()
    for read, write in zip(reads, writes):
        read.wait()
        write.start()
    for copy in writes:
        copy.wait()


def copied(*arrays):
    count = len(arrays)
    anywhere = pl.BlockSpec(memory_space=pl.ANY)
    return pl.pallas_call(
        functools.partial(copy_kernel, count),
        out_shape=tuple(jax.ShapeDtypeStruct(a.shape, a.dtype) for a in arrays),
        in_specs=[anywhere] * count,
        out_specs=(anywhere,) * count,
        scratch_shapes=[pltpu.VMEM(a.shape, a.dtype) for a in arrays]
        + [pltpu.SemaphoreType.DMA((count, 2)), pltpu.SemaphoreType.DMA((count, 2))],
        compiler_params=pltpu.CompilerParams(vmem_limit_bytes=60 * MIB),
        name="results",
    )(*arrays)


def local(primal, tangent, cotangent, impulse):
    length = impulse.shape[0]
    tables = [jnp.asarray(t) for t in build_tables(length)]
    scale = 1.0 / math.sqrt(lax.axis_size("dp") * length)
    back_u, back_g, back_du, summed = copied(*fused(primal, cotangent, tangent, impulse, tables, scale))
    return (back_u, back_du, back_g, summed)


def solution(mesh):
    placed = (P("dp", "ctx", None), P("dp", "ctx", None), P("dp", "ctx", None), P(None, "ctx"))
    return jax.shard_map(
        local,
        mesh=mesh,
        in_specs=placed,
        out_specs=(
            P("dp", "ctx", None),
            P("dp", "ctx", None),
            P("dp", "ctx", None),
            P(None, "ctx"),
        ),
        check_vma=False,
    )
```

```python
import functools
import math

import jax
import jax.numpy as jnp
import ml_dtypes
import numpy as np
from jax import lax
from jax.experimental import pallas as pl
from jax.experimental.pallas import tpu as pltpu
from jax.sharding import PartitionSpec as P

MESH = pl.DeviceIdType.MESH
LANES = 128
SPLIT = 16
MIB = 1024 * 1024
UNROLL = 16


def two_pieces(table):
    high = table.astype(ml_dtypes.bfloat16)
    low = (table - high.astype(np.float64)).astype(ml_dtypes.bfloat16)
    return high, low


def build_tables(length):
    total = 2 * length
    rows = length // SPLIT
    time = np.arange(rows)[None, :] * SPLIT + np.arange(SPLIT)[:, None]
    angle = 2.0 * np.pi * (time[:, None, :] * np.arange(rows)[None, :, None] % total) / total
    real, imag = np.cos(angle), -np.sin(angle)
    real[:, 0, :] = 1.0
    imag[:, 0, :] = 1.0 - 2.0 * (np.arange(rows) % 2)
    high, low = two_pieces(np.concatenate([real, imag], 1))
    analysis = np.concatenate([high, low], 2)
    real, imag = np.cos(angle) * (2.0 / total), -np.sin(angle) * (2.0 / total)
    real[:, 0, :] = (np.arange(rows) % 2 == 0)[None, :]
    imag[:, 0, :] = (np.arange(rows) % 2 == 1)[None, :]
    high, low = two_pieces(np.concatenate([real, imag], 1).transpose(0, 2, 1))
    synthesis = np.concatenate([high, low], 1)
    edge = np.zeros((2 * SPLIT, 2 * SPLIT))
    back = np.zeros((2 * SPLIT, 2 * SPLIT))
    point = np.arange(SPLIT)
    folded = np.arange(2 * SPLIT)
    for m in range(SPLIT):
        turn = 2.0 * np.pi * m * point / (2 * SPLIT)
        start = SPLIT * (m % 2)
        edge[m, start : start + SPLIT] = np.cos(turn)
        full = 2.0 * np.pi * m * folded / (2 * SPLIT)
        if m:
            edge[SPLIT + m, start : start + SPLIT] = -np.sin(turn)
            back[:, m] = 2.0 * np.cos(full) / total
            back[:, SPLIT + m] = -2.0 * np.sin(full) / total
    edge[SPLIT, :SPLIT] = np.cos(np.pi * point)
    back[:, 0] = 1.0 / total
    back[:, SPLIT] = np.cos(np.pi * folded) / total
    return analysis, synthesis, edge.astype(np.float32), back.astype(np.float32)


def times(value, power, sign):
    re, im = value
    power = (power * sign) % 16
    if power == 0:
        return (re, im)
    if power == 4:
        return (-im, re)
    if power == 8:
        return (-re, -im)
    if power == 12:
        return (im, -re)
    c, s = math.cos(math.pi * power / 8), math.sin(math.pi * power / 8)
    if power % 4 == 2:
        size = math.sqrt(0.5)
        if power == 2:
            return ((re - im) * size, (re + im) * size)
        if power == 6:
            return ((re + im) * -size, (re - im) * size)
        if power == 10:
            return ((im - re) * size, (re + im) * -size)
        return ((re + im) * size, (im - re) * size)
    return (re * c - im * s, re * s + im * c)


def four(a, b, c, d, sign):
    sr, si = a[0] + c[0], a[1] + c[1]
    dr, di = a[0] - c[0], a[1] - c[1]
    tr, ti = b[0] + d[0], b[1] + d[1]
    er, ei = b[0] - d[0], b[1] - d[1]
    plus = (dr - ei, di + er)
    minus = (dr + ei, di - er)
    if sign < 0:
        plus, minus = minus, plus
    return ((sr + tr, si + ti), plus, (sr - tr, si - ti), minus)


def sixteen(points, sign):
    inner = [four(points[b], points[4 + b], points[8 + b], points[12 + b], sign) for b in range(4)]
    result = [None] * 16
    for c in range(4):
        column = [times(inner[b][c], b * c, sign) for b in range(4)]
        outer = four(*column, sign)
        for d in range(4):
            result[c + 4 * d] = outer[d]
    return result


def product(a, b, conjugate):
    if conjugate:
        return (a[0] * b[0] + a[1] * b[1], a[0] * b[1] - a[1] * b[0])
    return (a[0] * b[0] - a[1] * b[1], a[0] * b[1] + a[1] * b[0])


U, G, DU, H = range(4)
GRAD = 3
SUBS = 2


def encode(total, index, piece, value):
    top = jnp.max(jnp.abs(value), axis=0, keepdims=True).astype(jnp.bfloat16)
    size = top.astype(jnp.float32)
    scaled = value * jnp.where(size > 0.0, 1.0 / size, 0.0)
    fourth = (scaled * scaled) * (scaled * scaled) * 2.0**60
    code = fourth * fourth
    code = jnp.where(scaled < 0.0, -code, code)
    total[index, piece, : value.shape[0]] = code.astype(jnp.bfloat16)
    total[index, piece, value.shape[0] :] = jnp.broadcast_to(top, (16, top.shape[1]))


def decoded(total, index, piece):
    rows = total.shape[2] - 16
    code = total[index, piece, :rows].astype(jnp.float32)
    size = total[index, piece, rows:].astype(jnp.float32)[0:1]
    root = jnp.sqrt(jnp.sqrt(jnp.sqrt(jnp.abs(code)) * 2.0**-60))
    return jnp.where(code < 0.0, -root, root) * size


def fused_kernel(
    n, rings, scale,
    u_ref, g_ref, du_ref, h_ref, analysis_ref, synthesis_ref, edge, back,
    ou_ref, og_ref, odu_ref, grad_ref,
    arrive, leave, impulse, analysis, synthesis, signal, spec, prod, rim, rim_spec, rim_mix, rim_out,
    part, right_box, left_box, right_leaf, left_leaf, landing, total,
    table_sem, local_sem, in_send, in_recv, out_send, out_recv, sum_send, sum_recv, leaf_send, leaf_recv, land_send, land_recv,
    all_send, all_recv, near_send, near_recv, twin_sem,
):
    me, dp = lax.axis_index("ctx"), lax.axis_index("dp")
    z, x = lax.div(dp, 2), lax.rem(dp, 2)
    up, up_two, down, down_two = (
        {"dp": lax.rem(z + move, rings) * 2 + x} for move in (1, 2, rings - 1, rings - 2)
    )
    twin = {"dp": z * 2 + 1 - x}
    around = [
        {"dp": lax.rem(z + move, rings) * 2 + 1 - x} for move in (1, 2, rings - 1, rings - 2)
    ]
    length = impulse.shape[0]
    rows = length // SPLIT
    tokens = length // n
    steps = rings // 4
    sub = rows // SUBS
    mine = pl.ds(pl.multiple_of(me * tokens, tokens), tokens)
    own = pl.ds(pl.multiple_of(me * LANES, LANES), LANES)

    tables = [
        pltpu.make_async_copy(src, dst, table_sem.at[i])
        for i, (src, dst) in enumerate(((h_ref, impulse), (analysis_ref, analysis), (synthesis_ref, synthesis)))
    ]
    barrier = pltpu.get_barrier_semaphore()
    for step in range(1, n):
        pl.semaphore_signal(
            barrier, inc=1, device_id={"ctx": lax.rem(me + step, n)}, device_id_type=MESH
        )
    for device in (up, up_two, down, down_two, twin, *around):
        pl.semaphore_signal(barrier, inc=1, device_id=device, device_id_type=MESH)
    for copy in tables:
        copy.start()
    pl.semaphore_wait(barrier, n + 8)

    remote, sent, locals_ = {}, [], {}

    def send_in(s):
        src = (u_ref, g_ref, du_ref)[s]
        remote[s] = []
        for step in range(1, n):
            other = lax.rem(me + step, n)
            copy = pltpu.make_async_remote_copy(
                src_ref=src.at[0, :, pl.ds(pl.multiple_of(other * LANES, LANES), LANES)],
                dst_ref=arrive.at[s, mine, :],
                send_sem=in_send.at[s, step], recv_sem=in_recv.at[s, step],
                device_id={"ctx": other}, device_id_type=MESH,
            )
            copy.start()
            remote[s].append(copy)
        locals_[s] = pltpu.make_async_copy(src.at[0, :, own], arrive.at[s, mine, :], local_sem.at[s])
        locals_[s].start()

    def receive(s):
        for copy in remote[s]:
            copy.wait_recv()
        locals_[s].wait()
        sent.extend(remote[s])

    finished = []

    def send_out(o):
        dst = (ou_ref, og_ref, odu_ref)[o]
        for step in range(1, n):
            other = lax.rem(me + step, n)
            copy = pltpu.make_async_remote_copy(
                src_ref=leave.at[o, pl.ds(pl.multiple_of(other * tokens, tokens), tokens), :],
                dst_ref=dst.at[0, :, own],
                send_sem=out_send.at[o, step], recv_sem=out_recv.at[o, step],
                device_id={"ctx": other}, device_id_type=MESH,
            )
            copy.start()
            finished.append(copy)
        copy = pltpu.make_async_copy(leave.at[o, mine, :], dst.at[0, :, own], local_sem.at[3 + o])
        copy.start()
        finished.append(copy)

    def analyse(s, slots):
        def body(q, carry):
            pieces = [signal[i, pl.ds(q, rows, stride=SPLIT), :].astype(jnp.bfloat16) for i in slots]
            block = jnp.concatenate(pieces, 1) if len(slots) > 1 else pieces[0]
            block = jnp.concatenate([block, block], 0)
            out = jnp.dot(analysis[q], block, preferred_element_type=jnp.float32)
            if len(slots) > 1:
                out = out[:, :LANES] + out[:, LANES:]
            spec[s, q] = out
            rim[pl.ds(q, 1), :] = out[0:1]
            rim[pl.ds(SPLIT + q, 1), :] = out[rows : rows + 1]
            return carry

        lax.fori_loop(0, SPLIT, body, 0, unroll=UNROLL)
        rim_spec[s] = jnp.dot(
            edge[...], rim[...], precision=lax.Precision.HIGHEST, preferred_element_type=jnp.float32
        )

    def mix(o, a, b, conjugate, turned, kept):
        left, right = (rim_spec[a, :SPLIT], rim_spec[a, SPLIT:]), (rim_spec[b, :SPLIT], rim_spec[b, SPLIT:])
        re, im = product(left, right, conjugate)
        first = lax.broadcasted_iota(jnp.int32, (SPLIT, LANES), 0) == 0
        rim_mix[:SPLIT] = jnp.where(first, left[0] * right[0], re)
        rim_mix[SPLIT:] = jnp.where(first, left[1] * right[1], im)
        rim_out[o] = jnp.dot(
            back[...], rim_mix[...], precision=lax.Precision.HIGHEST, preferred_element_type=jnp.float32
        )

        def body(tile, carry):
            upper = pl.ds(pl.multiple_of(tile * 8, 8), 8)
            lower = pl.ds(pl.multiple_of(rows + tile * 8, 8), 8)
            points = [(spec[b, j, upper, :], spec[b, j, lower, :]) for j in range(SPLIT)]
            if not turned:
                points = sixteen(points, -1)
                if kept:
                    for j in range(SPLIT):
                        spec[b, j, upper, :] = points[j][0]
                        spec[b, j, lower, :] = points[j][1]
            points = [
                product((spec[a, j, upper, :], spec[a, j, lower, :]), points[j], conjugate)
                for j in range(SPLIT)
            ]
            points = sixteen(points, 1)
            for q in range(SPLIT):
                prod[o, q, upper, :] = points[q][0]
                prod[o, q, lower, :] = points[q][1]
            return carry

        lax.fori_loop(0, rows // 8, body, 0, unroll=2)

    def turn(s):
        def body(tile, carry):
            upper = pl.ds(pl.multiple_of(tile * 8, 8), 8)
            lower = pl.ds(pl.multiple_of(rows + tile * 8, 8), 8)
            points = sixteen([(spec[s, q, upper, :], spec[s, q, lower, :]) for q in range(SPLIT)], -1)
            for j in range(SPLIT):
                spec[s, j, upper, :] = points[j][0]
                spec[s, j, lower, :] = points[j][1]
            return carry

        lax.fori_loop(0, rows // 8, body, 0, unroll=2)

    def residue(o, q):
        prod[o, q, 0:1, :] = rim_out[o, pl.ds(q, 1), :]
        prod[o, q, rows : rows + 1, :] = rim_out[o, pl.ds(SPLIT + q, 1), :]
        block = prod[o, q]
        top = block.astype(jnp.bfloat16)
        rest = (block - top.astype(jnp.float32)).astype(jnp.bfloat16)
        both = jnp.dot(synthesis[q], top, preferred_element_type=jnp.float32)
        more = jnp.dot(synthesis[q, :rows], rest, preferred_element_type=jnp.float32)
        return both[:rows] + (both[rows:] + more)

    def finish(o):
        def body(q, carry):
            signal[o, pl.ds(q, rows, stride=SPLIT), :] = residue(o, q)
            return carry

        lax.fori_loop(0, SPLIT, body, 0, unroll=UNROLL)
        leave[o] = signal[o].astype(jnp.bfloat16)

    def load(s):
        signal[s] = arrive[s].astype(jnp.float32)

    def place(index):
        return lax.rem(index + 2 * rings, rings)

    started = []

    def hop(src, dst, sends, recvs, device):
        copy = pltpu.make_async_remote_copy(
            src_ref=src, dst_ref=dst, send_sem=sends, recv_sem=recvs, device_id=device, device_id_type=MESH
        )
        copy.start()
        started.append(copy)
        return copy

    cuts = [pl.ds(c * sub, sub) for c in range(SUBS)]

    send_in(U)
    send_in(G)
    tables[0].wait()
    high = impulse[...].astype(jnp.bfloat16).astype(jnp.float32)
    signal[0] = high
    signal[1] = impulse[...] - high
    tables[1].wait()
    analyse(H, (0, 1))
    turn(H)
    receive(U)
    load(U)
    analyse(U, (U,))
    turn(U)
    receive(G)
    load(G)
    analyse(G, (G,))
    mix(GRAD, U, G, True, False, True)
    tables[2].wait()

    def chunk(q):
        part[q] = residue(GRAD, q)

    def leaf(side, i):
        src, dst, device = (
            (part.at[place(z + 2 * steps - 1 - 2 * i)], right_leaf.at[i], up),
            (part.at[place(z - 2 * steps + 1 + 2 * i)], left_leaf.at[i], down),
        )[side]
        return hop(src, dst, leaf_send.at[side, i], leaf_recv.at[side, i], device)

    def chain(side, step, source):
        box, device = ((right_box, up_two), (left_box, down_two))[side]
        return [
            hop(source(c), box.at[step, c], sum_send.at[side, step, i], sum_recv.at[side, step, i], device)
            for i, c in enumerate(cuts)
        ]

    chunk(place(z + 2 * steps))
    right = chain(0, 0, lambda c: part.at[place(z + 2 * steps), c])
    chunk(place(z - 2 * steps + 1))
    left_leaves = [leaf(1, 0)]
    chunk(place(z + 2 * steps - 1))
    right_leaves = [leaf(0, 0)]

    def others(step, carry):
        chunk(place(z - 2 * steps + 1 + step))
        return carry

    lax.fori_loop(1, rings - 2, others, 0, unroll=rings - 3)
    left_leaves.append(leaf(1, 1))
    right_leaves.append(leaf(0, 1))

    def sum_left(step, left):
        left_leaves[step].wait_recv()
        q = place(z - 2 * steps + 2 + 2 * step)
        if step == 0:
            for c in cuts:
                left_leaf[0, c] += part[q, c]
            return chain(1, 0, lambda c: left_leaf.at[0, c])
        for i, c in enumerate(cuts):
            left[i].wait_recv()
            left_box[step - 1, c] += part[q, c] + left_leaf[step, c]
        if step == steps - 2:
            return land(1, rings - 2, lambda c: left_box.at[step - 1, c])
        return chain(1, step, lambda c: left_box.at[step - 1, c])

    def sum_right(step, right):
        right_leaves[step - 1].wait_recv()
        q = place(z + 2 * steps - 2 * step)
        for i, c in enumerate(cuts):
            right[i].wait_recv()
            right_box[step - 1, c] += part[q, c] + right_leaf[step - 1, c]
        if step == steps - 1:
            return land(0, 2, lambda c: right_box.at[step - 1, c])
        return chain(0, step, lambda c: right_box.at[step - 1, c])

    half = rows // 2
    kept = pl.ds(pl.multiple_of(x * half, half), half)
    given = pl.ds(pl.multiple_of((1 - x) * half, half), half)

    def land(kind, move, source):
        for rail in range(2):
            device = {"dp": lax.rem(z + move, rings) * 2 + rail}
            hop(
                source(pl.ds(rail * half, half)), landing.at[kind, x],
                land_send.at[kind, rail], land_recv.at[kind, x], device,
            )

    def landed(kind, rail):
        pltpu.make_async_remote_copy(
            src_ref=landing.at[kind, rail], dst_ref=landing.at[kind, rail],
            send_sem=land_send.at[kind, rail], recv_sem=land_recv.at[kind, rail],
            device_id=twin, device_id_type=MESH,
        ).wait_recv()

    send_in(DU)
    left = sum_left(0, None)
    right = sum_right(1, right)
    left_leaves.append(leaf(1, 2))
    right_leaves.append(leaf(0, 2))
    mix(U, H, U, False, True, False)
    finish(U)
    left = sum_left(1, left)
    right = sum_right(2, right)
    gift = hop(part.at[z, given], landing.at[4, 0], land_send.at[4, 0], land_recv.at[4, 0], twin)
    land(2, 1, lambda c: part.at[place(z + 1), c])
    land(3, rings - 1, lambda c: part.at[place(z - 1), c])
    send_out(U)
    mix(G, H, G, True, True, False)
    sum_left(2, left)
    sum_right(3, right)
    finish(G)
    receive(DU)
    load(DU)
    analyse(DU, (DU,))
    gift.wait_recv()
    mine_sum = part[z, kept] + landing[4, 0]
    for kind in (2, 3, 1, 0):
        for rail in range(2):
            landed(kind, rail)
        mine_sum = mine_sum + (landing[kind, 0] + landing[kind, 1])
    encode(total, z, x, mine_sum)

    streams = (x, 1 - x)

    def spread(side, step, i, last_chain):
        index = place(z - 2 * step) if side == 0 else place(z + 2 * step)
        two, one = ((up_two, up), (down_two, down))[side]
        here = total.at[index, streams[i]]
        first = None
        if not last_chain:
            first = hop(here, here, all_send.at[side, step, i], all_recv.at[side, step, i], two)
        return first, hop(here, here, near_send.at[side, step, i], near_recv.at[side, step, i], one)

    def decode(q):
        for part_of in range(2):
            grad_ref[pl.ds(q + part_of * half * SPLIT, half, stride=SPLIT), :] = decoded(total, q, part_of) * scale

    here = total.at[z, x]
    swap = hop(here, here, twin_sem.at[0], twin_sem.at[1], twin)
    far, near = {}, {}
    for i in range(2):
        if i:
            swap.wait_recv()
        for side in range(2):
            far[side, i], near[side, i] = spread(side, 0, i, False)
    send_out(G)
    mix(DU, H, DU, False, False, False)
    decode(z)
    for step in range(1, steps):
        behind = dict(near)
        for i in range(2):
            for side in range(2):
                far[side, i].wait_recv()
                far[side, i], near[side, i] = spread(side, step, i, side == 1 and step == steps - 1)
        if step == 1:
            finish(DU)
            send_out(DU)
        decode(place(z - 2 * step))
        decode(place(z + 2 * step))
        for side in range(2):
            for i in range(2):
                behind[side, i].wait_recv()
            decode(place(z - 2 * step + 1) if side == 0 else place(z + 2 * step - 1))
    for i in range(2):
        far[0, i].wait_recv()
    decode(place(z - 2 * steps))
    for side in range(2):
        for i in range(2):
            near[side, i].wait_recv()
        decode(place(z - 2 * steps + 1) if side == 0 else place(z + 2 * steps - 1))
    for copy in started + sent:
        copy.wait_send()
    for copy in finished:
        copy.wait()


def fused(u, g, du, h, tables, scale):
    n = lax.axis_size("ctx")
    rings = lax.axis_size("dp") // 2
    length, width = h.shape
    rows = length // SPLIT
    steps = rings // 4
    anywhere = pl.BlockSpec(memory_space=pl.ANY)
    whole = pl.BlockSpec(memory_space=pltpu.VMEM)
    shape = jax.ShapeDtypeStruct((1, length // n, n * width), jnp.bfloat16)
    sem = pltpu.SemaphoreType.DMA

    def space(*sizes, kind=jnp.float32):
        return pltpu.VMEM(sizes, kind)

    half = jnp.bfloat16
    return pl.pallas_call(
        functools.partial(fused_kernel, n, rings, scale),
        out_shape=(shape,) * 3 + (jax.ShapeDtypeStruct((length, width), jnp.float32),),
        in_specs=[anywhere] * 6 + [whole] * 2,
        out_specs=(anywhere,) * 3 + (whole,),
        scratch_shapes=[
            space(3, length, width, kind=half),
            space(3, length, width, kind=half),
            space(length, width),
            space(*tables[0].shape, kind=half),
            space(*tables[1].shape, kind=half),
            space(3, length, width),
            space(4, SPLIT, 2 * rows, width),
            space(4, SPLIT, 2 * rows, width),
            space(2 * SPLIT, width),
            space(4, 2 * SPLIT, width),
            space(2 * SPLIT, width),
            space(4, 2 * SPLIT, width),
            space(rings, rows, width),
            space(steps - 1, rows, width),
            space(steps - 1, rows, width),
            space(steps - 1, rows, width),
            space(steps - 1, rows, width),
            space(5, 2, rows // 2, width),
            space(rings, 2, rows // 2 + 16, width, kind=half),
            sem((3,)), sem((6,)),
            sem((3, n)), sem((3, n)), sem((3, n)), sem((3, n)),
            sem((2, steps, SUBS)), sem((2, steps, SUBS)), sem((2, steps)), sem((2, steps)), sem((5, 2)), sem((5, 2)),
            sem((2, steps, 2)), sem((2, steps, 2)), sem((2, steps, 2)), sem((2, steps, 2)), sem((2,)),
        ],
        compiler_params=pltpu.CompilerParams(
            collective_id=0, has_side_effects=True, vmem_limit_bytes=60 * MIB
        ),
        name="hyena",
    )(u, g, du, h, *tables)


def copy_kernel(count, *refs):
    sources, targets, staged = refs[:count], refs[count : 2 * count], refs[2 * count : 3 * count]
    read_sem, write_sem = refs[3 * count :]
    reads, writes = [], []
    for i in range(count):
        for piece in range(2):
            size = sources[i].shape[-2] // 2
            cut = (0,) * (len(sources[i].shape) - 2) + (pl.ds(piece * size, size),)
            source, middle, target = sources[i].at[cut], staged[i].at[cut], targets[i].at[cut]
            reads.append(pltpu.make_async_copy(source, middle, read_sem.at[i, piece]))
            writes.append(pltpu.make_async_copy(middle, target, write_sem.at[i, piece]))
    for copy in reads:
        copy.start()
    for read, write in zip(reads, writes):
        read.wait()
        write.start()
    for copy in writes:
        copy.wait()


def copied(*arrays):
    count = len(arrays)
    anywhere = pl.BlockSpec(memory_space=pl.ANY)
    return pl.pallas_call(
        functools.partial(copy_kernel, count),
        out_shape=tuple(jax.ShapeDtypeStruct(a.shape, a.dtype) for a in arrays),
        in_specs=[anywhere] * count,
        out_specs=(anywhere,) * count,
        scratch_shapes=[pltpu.VMEM(a.shape, a.dtype) for a in arrays]
        + [pltpu.SemaphoreType.DMA((count, 2)), pltpu.SemaphoreType.DMA((count, 2))],
        compiler_params=pltpu.CompilerParams(vmem_limit_bytes=60 * MIB),
        name="results",
    )(*arrays)


def local(primal, tangent, cotangent, impulse):
    length = impulse.shape[0]
    tables = [jnp.asarray(t) for t in build_tables(length)]
    scale = 1.0 / math.sqrt(lax.axis_size("dp") * length)
    back_u, back_g, back_du, summed = copied(*fused(primal, cotangent, tangent, impulse, tables, scale))
    return (back_u, back_du, back_g, summed)


def solution(mesh):
    placed = (P("dp", "ctx", None), P("dp", "ctx", None), P("dp", "ctx", None), P(None, "ctx"))
    return jax.shard_map(
        local,
        mesh=mesh,
        in_specs=placed,
        out_specs=(
            P("dp", "ctx", None),
            P("dp", "ctx", None),
            P("dp", "ctx", None),
            P(None, "ctx"),
        ),
        check_vma=False,
    )
```
